128 devices in a mesh: head: 8 (over x_lo, z), wide: 16 (over x_hi, y, core).
Axes of the slice: x: 4 (x_hi: 2, x_lo: 2; x = x_hi * 2 + x_lo), y: 4, z: 4, core: 2. Of those that a mesh axis runs over, the one named last changes fastest.
Arguments:
- queries: bfloat16 [1024, 8192], P('wide', 'head'), may hold values from -16 to 16
- fresh_keys: bfloat16 [1024, 1024], P('wide', 'head'), may hold values from -16 to 16
- fresh_values: bfloat16 [1024, 1024], P('wide', 'head'), may hold values from -5 to 5
- cached_keys: bfloat16 [16, 2048, 1024], P('wide', None, 'head'), may hold values from -10 to 10
- cached_values: bfloat16 [16, 2048, 1024], P('wide', None, 'head'), may hold values from -5 to 5
- context_len: int32 [16], P('wide'), may hold values from 512 to 2048, as said below
- tree_size: int32 [16], P('wide'), may hold values from 16 to 64, as said below
- parents: int32 [16, 64], P('wide'), may hold values from 0 to 62, as said below
- residual: bfloat16 [1024, 8192], P(None, 'wide'), may hold values from -36 to 36
- out_weight: bfloat16 [8192, 8192], P('head', 'wide'), may hold values from -0.0625 to 0.0625
- gate_up_weight: bfloat16 [8192, 2, 28672], P('wide', None, 'head'), may hold values from -0.0625 to 0.0625
- down_weight: bfloat16 [28672, 8192], P('head', 'wide'), may hold values from -0.03125 to 0.03125
Outputs:
- attended: bfloat16 [1024, 8192], P('head', 'wide')
- update: bfloat16 [1024, 8192], P('head', 'wide')
The draws below stay inside these ranges and needn't reach their ends.
Inputs may be any that keep to these rules, and one draw needn't show every extreme that they name: `context_len`: some request has exactly 2048. `tree_size`: a multiple of 16; some request has exactly 64. `parents`: node 0 is each tree's root and its own parent; every other node's parent is an earlier node.
All inputs are finite; a program needn't handle non-finite values.
Results may differ from the reference program's by a relative error of at most 0.035.
Values may be sent and summed in bfloat16 or wider, within the bound.
A program may use at most 128 MiB of HBM per device.

```python
import math
import jax
import jax.numpy as jnp
from jax import lax

D = 8192
HEADS = 64
KV = 8
HD = 128
FF = 28672
TREE = 64
CTX = 2048
REQS = 16
TOKENS = 1024
N_HEAD = 8
N_WIDE = 16


def tree_pattern(key):
    gauss = jax.random.truncated_normal(jax.random.fold_in(key, 1), -4.0, 4.0, (TOKENS, KV * HD), jnp.float32)
    return 4.0 * gauss


def draw_fresh_keys(key, part):
    shared = tree_pattern(key)
    return shared.astype(jnp.bfloat16)


def draw_queries(key, part):
    groups = HEADS // KV
    key = jax.random.fold_in(key, 12)
    result = jax.random.truncated_normal(key, -4.0, 4.0, (REQS, TREE, KV, groups, HD), jnp.float32)
    return result.reshape(TOKENS, HEADS * HD).astype(jnp.bfloat16)


def draw_residual(key, part):
    key = jax.random.fold_in(key, 13)
    first, second, third = jax.random.split(key, 3)
    row_scales = jnp.exp(jax.random.uniform(first, (TOKENS, 1), jnp.float32, jnp.log(0.3), jnp.log(3.0)))
    column_scales = jnp.exp(jax.random.uniform(second, (1, D), jnp.float32, jnp.log(0.3), jnp.log(3.0)))
    basis = jax.random.truncated_normal(third, -4.0, 4.0, (TOKENS, D), jnp.float32)
    return (basis * row_scales * column_scales).astype(jnp.bfloat16)


def draw_parents(key, part):
    key = jax.random.fold_in(key, 14)
    node_ids = jnp.arange(TREE, dtype=jnp.int32)[None, :]
    lowest = jnp.maximum(node_ids - 4, 0)
    highest = jnp.maximum(node_ids, 1)
    picked = jax.random.randint(key, (REQS, TREE), lowest, highest, jnp.int32)
    picked = jnp.where(node_ids == 0, 0, picked)
    picked = jnp.where(node_ids == TREE - 1, TREE - 2, picked)
    return picked.astype(jnp.int32)


def draw_context_len(key, part):
    key = jax.random.fold_in(key, 15)
    first, second = jax.random.split(key)
    lengths = jax.random.randint(first, (REQS,), CTX // 4, CTX + 1, jnp.int32)
    longest = jax.random.randint(second, (), 0, REQS, jnp.int32)
    return jnp.where(jnp.arange(REQS, dtype=jnp.int32) == longest, CTX, lengths).astype(jnp.int32)


def draw_tree_size(key, part):
    key = jax.random.fold_in(key, 16)
    first, second = jax.random.split(key)
    sizes = jax.random.randint(first, (REQS,), 1, TREE // 16 + 1, jnp.int32) * 16
    fullest = jax.random.randint(second, (), 0, REQS, jnp.int32)
    return jnp.where(jnp.arange(REQS, dtype=jnp.int32) == fullest, TREE, sizes).astype(jnp.int32)


def level_of(own_key, shape, cuts, low, largest):
    gain = 1.0
    for axis_at, blocks in cuts:
        heights = jax.random.uniform(jax.random.fold_in(jax.random.fold_in(own_key, 6), axis_at), (blocks,), jnp.float32, low / len(cuts), largest / len(cuts))
        gain = gain * jnp.repeat(jnp.exp(heights), shape[axis_at] // blocks).reshape((-1,) + (1,) * (len(shape) - 1 - axis_at))
    return gain


def noise(stream_key, shape, scale, reach, shards=(), kind=jnp.bfloat16):
    loudness = level_of(stream_key, shape, shards, -0.22, 0.18) if shards else 1.0
    values = jax.random.normal(stream_key, shape, jnp.float32) * scale * loudness
    return jnp.minimum(jnp.maximum(values, -reach), reach).astype(kind)


def setup_inputs(seed: int = 0) -> dict:
    arg_keys = jax.random.split(jax.random.key(seed), 13)
    return {
        "queries": draw_queries(jax.random.fold_in(arg_keys[12], 71), 0),
        "fresh_keys": draw_fresh_keys(jax.random.fold_in(arg_keys[12], 71), 0),
        "fresh_values": noise(arg_keys[2], (TOKENS, KV * HD), 1.0, 5.0, ((0, 16), (1, 8))),
        "cached_keys": noise(arg_keys[3], (REQS, CTX, KV * HD), 2.5, 10.0, ((0, 16), (2, 8))),
        "cached_values": noise(arg_keys[4], (REQS, CTX, KV * HD), 1.0, 5.0, ((0, 16), (2, 8))),
        "context_len": draw_context_len(jax.random.fold_in(arg_keys[12], 71), 0),
        "tree_size": draw_tree_size(jax.random.fold_in(arg_keys[12], 71), 0),
        "parents": draw_parents(jax.random.fold_in(arg_keys[12], 71), 0),
        "residual": draw_residual(jax.random.fold_in(arg_keys[12], 71), 0),
        "out_weight": noise(arg_keys[9], (HEADS * HD, D), (HEADS * HD) ** -0.5, 0.0625, ((0, 8), (1, 16))),
        "gate_up_weight": noise(arg_keys[10], (D, 2, FF), D ** -0.5, 0.0625, ((0, 16), (2, 8))),
        "down_weight": noise(arg_keys[11], (FF, D), FF ** -0.5, 0.03125, ((0, 8), (1, 16))),
    }


epsilon = 1e-05

def ancestry(parent_row, node_count):
    node_ids = jnp.arange(node_count, dtype=jnp.int32)
    linked = (parent_row[:, None] == node_ids[None, :]) | (node_ids[:, None] == node_ids[None, :])
    reached = linked.astype(jnp.float32)
    for squaring in range(max(1, (node_count - 1).bit_length())):
        reached = jnp.minimum(jnp.dot(reached, reached, precision=lax.Precision.HIGHEST), 1.0)
    return reached > 0.5

def attend_request(query_block, cache_keys, cache_values, tree_keys, tree_values, length, live_count, parent_row):
    node_count = query_block.shape[0]
    score_scale = 1.0 / math.sqrt(query_block.shape[-1])
    visible = ancestry(parent_row, node_count)
    positions = jnp.arange(cache_keys.shape[0], dtype=jnp.int32)
    node_ids = jnp.arange(node_count, dtype=jnp.int32)
    cache_open = positions < length
    tree_open = visible & (node_ids[None, :] < live_count)
    cache_scores = jnp.einsum('tkgd,ckd->kgtc', query_block, cache_keys) * score_scale
    tree_scores = jnp.einsum('tkgd,ukd->kgtu', query_block, tree_keys) * score_scale
    cache_scores = jnp.where(cache_open[None, None, None, :], cache_scores, -1e+30)
    tree_scores = jnp.where(tree_open[None, None], tree_scores, -1e+30)
    row_max = jnp.maximum(lax.optimization_barrier(jnp.max(cache_scores, axis=-1)), lax.optimization_barrier(jnp.max(tree_scores, axis=-1)))
    cache_probs = jnp.exp(cache_scores - row_max[..., None])
    tree_probs = jnp.exp(tree_scores - row_max[..., None])
    denominator = lax.optimization_barrier(jnp.sum(cache_probs, axis=-1)) + lax.optimization_barrier(jnp.sum(tree_probs, axis=-1))
    cache_weights = lax.optimization_barrier(cache_probs.astype(jnp.bfloat16)).astype(jnp.float32)
    tree_weights = lax.optimization_barrier(tree_probs.astype(jnp.bfloat16)).astype(jnp.float32)
    gathered = jnp.einsum('kgtc,ckd->tkgd', cache_weights, cache_values) + jnp.einsum('kgtu,ukd->tkgd', tree_weights, tree_values)
    result = gathered / jnp.transpose(denominator, (2, 0, 1))[..., None]
    live_rows = node_ids < live_count
    return jnp.where(live_rows[:, None, None, None], result, 0.0)

def reference(queries, fresh_keys, fresh_values, cached_keys, cached_values, context_len, tree_size, parents, residual, out_weight, gate_up_weight, down_weight):
    groups = HEADS // KV
    query_all = queries.astype(jnp.float32).reshape(REQS, TREE, KV, groups, HD)
    cache_k = cached_keys.astype(jnp.float32).reshape(REQS, CTX, KV, HD)
    cache_v = cached_values.astype(jnp.float32).reshape(REQS, CTX, KV, HD)
    tree_k = fresh_keys.astype(jnp.float32).reshape(REQS, TREE, KV, HD)
    tree_v = fresh_values.astype(jnp.float32).reshape(REQS, TREE, KV, HD)

    def per_request(request_items):
        return attend_request(*request_items)
    attention = lax.map(per_request, (query_all, cache_k, cache_v, tree_k, tree_v, context_len, tree_size, parents))
    attention_rows = attention.reshape(TOKENS, HEADS * HD).astype(jnp.bfloat16)
    per_group = HEADS * HD // N_HEAD
    projection = jnp.zeros((TOKENS, D), jnp.float32)
    for group_index in range(N_HEAD):
        partial_value = jnp.dot(attention_rows[:, group_index * per_group:(group_index + 1) * per_group], out_weight[group_index * per_group:(group_index + 1) * per_group], preferred_element_type=jnp.float32)
        projection = projection + lax.optimization_barrier(partial_value.astype(jnp.bfloat16)).astype(jnp.float32)
    combined = residual.astype(jnp.float32) + projection
    attended = combined.astype(jnp.bfloat16)
    squares = lax.optimization_barrier(jnp.sum(combined * combined, axis=1, keepdims=True))
    normed = (combined * lax.rsqrt(squares / D + epsilon)).astype(jnp.bfloat16)
    stacked = gate_up_weight.reshape(D, 2 * FF)
    per_block = D // N_WIDE
    gate_up = jnp.zeros((TOKENS, 2 * FF), jnp.float32)
    for block_index in range(N_WIDE):
        partial_value = jnp.dot(normed[:, block_index * per_block:(block_index + 1) * per_block], stacked[block_index * per_block:(block_index + 1) * per_block], preferred_element_type=jnp.float32)
        gate_up = gate_up + lax.optimization_barrier(partial_value.astype(jnp.bfloat16)).astype(jnp.float32)
    hidden = (jax.nn.silu(gate_up[:, :FF]) * gate_up[:, FF:]).astype(jnp.bfloat16)
    update = jnp.dot(hidden, down_weight, preferred_element_type=jnp.float32).astype(jnp.bfloat16)
    return (attended, update)
```

```python
import functools
import math

import jax
import jax.numpy as jnp
from jax import lax
from jax.experimental import pallas as pl
from jax.experimental.pallas import tpu as pltpu
from jax.sharding import PartitionSpec as P

D = 8192
HEADS = 64
KV = 8
HD = 128

epsilon = 1e-05

BF = jnp.bfloat16
F32 = jnp.float32
MESH = pl.DeviceIdType.MESH

A_U = 512
B_U = 384
A_W = 2 * A_U
B_W = 2 * B_U
HALF = 2 * A_U + 2 * B_U
H_OFF = (0, A_U, 2 * A_U, 2 * A_U + B_U)


def ancestry(parent_row, node_count):
    node_ids = jnp.arange(node_count, dtype=jnp.int32)
    linked = (parent_row[:, None] == node_ids[None, :]) | (node_ids[:, None] == node_ids[None, :])
    reached = linked.astype(jnp.float32)
    for squaring in range(max(1, (node_count - 1).bit_length())):
        reached = jnp.minimum(jnp.dot(reached, reached, precision=lax.Precision.HIGHEST), 1.0)
    return reached > 0.5


def attend_request(
    query_block, cache_keys, cache_values, tree_keys, tree_values, length, live_count, parent_row
):
    node_count = query_block.shape[0]
    score_scale = 1.0 / math.sqrt(query_block.shape[-1])
    visible = ancestry(parent_row, node_count)
    positions = jnp.arange(cache_keys.shape[0], dtype=jnp.int32)
    node_ids = jnp.arange(node_count, dtype=jnp.int32)
    cache_open = positions < length
    tree_open = visible & (node_ids[None, :] < live_count)
    cache_scores = (
        jnp.einsum("tkgd,ckd->kgtc", query_block, cache_keys, preferred_element_type=jnp.float32)
        * score_scale
    )
    tree_scores = (
        jnp.einsum("tkgd,ukd->kgtu", query_block, tree_keys, preferred_element_type=jnp.float32)
        * score_scale
    )
    cache_scores = jnp.where(cache_open[None, None, None, :], cache_scores, -1e30)
    tree_scores = jnp.where(tree_open[None, None], tree_scores, -1e30)
    row_max = jnp.maximum(jnp.max(cache_scores, axis=-1), jnp.max(tree_scores, axis=-1))
    cache_probs = jnp.exp(cache_scores - row_max[..., None])
    tree_probs = jnp.exp(tree_scores - row_max[..., None])
    denominator = jnp.sum(cache_probs, axis=-1) + jnp.sum(tree_probs, axis=-1)
    gathered = jnp.einsum(
        "kgtc,ckd->tkgd",
        cache_probs.astype(jnp.bfloat16),
        cache_values,
        preferred_element_type=jnp.float32,
    )
    gathered = gathered + jnp.einsum(
        "kgtu,ukd->tkgd",
        tree_probs.astype(jnp.bfloat16),
        tree_values,
        preferred_element_type=jnp.float32,
    )
    result = gathered / jnp.transpose(denominator, (2, 0, 1))[..., None]
    live_rows = node_ids < live_count
    return jnp.where(live_rows[:, None, None, None], result, 0.0)


def layer_kernel(
    att, gw, dw, wo_hbm, res_hbm,
    att_out, upd_out,
    G, R0, R1, WC, DD, WO, RES, PP, RB, X, PA, PB, RA, RAX, RBX, RBY, SQ, SQR, H, PDO, PDS, PDI, FR,
    lsem, ssem, rsem,
):
    h = lax.axis_index("head")
    w = lax.axis_index("wide")
    xh = w // 8
    y = (w // 2) % 4
    c = w % 2

    def wide(dxh, dy):
        return (((xh + dxh) % 2) * 4 + (y + dy + 4) % 4) * 2 + c

    sib = (h, w + 1 - 2 * c)

    def wdev(dxh, dy):
        return (h, wide(dxh, dy))

    def hdev(k):
        return ((h + k) % 8, w)

    names = {}
    sent = []

    def send(name, src, dst, dev):
        i = names.setdefault(name, len(names))
        cp = pltpu.make_async_remote_copy(
            src_ref=src, dst_ref=dst, send_sem=ssem.at[i], recv_sem=rsem.at[i],
            device_id=dev, device_id_type=MESH,
        )
        cp.start()
        sent.append(cp)

    def arrive(name, dst, dev):
        i = names[name]
        pltpu.make_async_remote_copy(
            src_ref=dst, dst_ref=dst, send_sem=ssem.at[i], recv_sem=rsem.at[i],
            device_id=dev, device_id_type=MESH,
        ).wait_recv()

    mine = pl.ds(pl.multiple_of(c * HALF, 128), HALF)
    other = pl.ds(pl.multiple_of((1 - c) * HALF, 128), HALF)
    loads = [
        pltpu.make_async_copy(wo_hbm, WO, lsem.at[0]),
        pltpu.make_async_copy(gw.at[:, :, mine], R0, lsem.at[1]),
        pltpu.make_async_copy(dw.at[mine, :], DD.at[0], lsem.at[2]),
        pltpu.make_async_copy(
            res_hbm.at[pl.ds(pl.multiple_of(h * 128, 128), 128), :], RES, lsem.at[3]
        ),
    ]
    for cp in loads:
        cp.start()

    partners = [sib]
    partners += [wdev(dx, dy) for dx in range(2) for dy in range(4) if (dx, dy) != (0, 0)]
    partners += [hdev(k) for k in range(1, 8)]
    barrier = pltpu.get_barrier_semaphore()
    for dev in partners:
        pl.semaphore_signal(barrier, inc=1, device_id=dev, device_id_type=MESH)
    pl.semaphore_wait(barrier, len(partners))

    send("g_x", att, G.at[w], wdev(1, 0))
    for dy in (1, 3, 2):
        send(f"g_y{dy}", att, G.at[w], wdev(0, dy))
    send("g_c", att, G.at[w], sib)
    send("s_gw", gw.at[:, :, other], R1, sib)
    send("s_dw", dw.at[other, :], DD.at[1], sib)
    G[w] = att[...]

    def untwist(raw, row0, lo, hi):
        @pl.loop(lo, hi)
        def _(i):
            r = pl.ds(pl.multiple_of(i * 64, 64), 64)
            o = pl.ds(pl.multiple_of(row0 + i * 64, 64), 64)
            b = raw[r]
            gate, up = b[:, 0, :], b[:, 1, :]
            for p in range(4):
                n = A_U if p < 2 else B_U
                u = H_OFF[p]
                WC[o, 2 * u : 2 * u + n] = gate[:, u : u + n]
                WC[o, 2 * u + n : 2 * u + 2 * n] = up[:, u : u + n]

    wxp = wide(1, 0)
    arrive("g_x", G.at[wxp], wdev(1, 0))
    for dy in (1, 3, 2):
        send(f"g_xy{dy}", G.at[wxp], G.at[wxp], wdev(0, dy))
    send("g_cx", G.at[wxp], G.at[wxp], sib)
    for dx, tag in ((0, "y"), (1, "xy")):
        for dy in (1, 3, 2):
            src = wide(dx, -dy)
            arrive(f"g_{tag}{dy}", G.at[src], wdev(0, -dy))
            send(f"g_c{tag}{dy}", G.at[src], G.at[src], sib)
    loads[1].wait()
    untwist(R0, 0, 0, 2)
    flip = 1 - 2 * c
    arrive("g_c", G.at[w + flip], sib)
    arrive("g_cx", G.at[wxp + flip], sib)
    for dx, tag in ((0, "y"), (1, "xy")):
        for dy in (1, 3, 2):
            arrive(f"g_c{tag}{dy}", G.at[wide(dx, -dy) + flip], sib)

    loads[0].wait()
    for k in range(1, 9):
        j = (h + k) % 8
        rows = G[pl.ds(2 * j, 2)].reshape(128, 1024)
        PP[j] = jnp.dot(rows, WO[...], preferred_element_type=F32).astype(BF)
        if k < 8:
            send(f"o_{k}", PP.at[j], RB.at[k - 1], hdev(k))
    untwist(R0, 0, 2, 8)
    arrive("s_gw", R1, sib)
    untwist(R1, 512, 0, 4)
    loads[3].wait()
    total = RES[...].astype(F32) + PP[h].astype(F32)
    for k in range(1, 8):
        arrive(f"o_{k}", RB.at[k - 1], hdev(-k + 8))
        total = total + RB[k - 1].astype(F32)
    rounded = total.astype(BF)
    att_out[...] = rounded
    X[h, :, 0:512] = rounded

    own = X.at[h, :, 0:512]
    for k in range(1, 8):
        send(f"x_{k}", own, own, hdev(k))
    send("x_c", own, X.at[h, :, 512:1024], sib)
    untwist(R1, 512, 4, 8)
    for k in range(1, 8):
        j = (h + 8 - k) % 8
        arrive(f"x_{k}", X.at[j, :, 0:512], hdev(8 - k))
        send(f"x_c{k}", X.at[j, :, 0:512], X.at[j, :, 512:1024], sib)
    arrive("x_c", X.at[h, :, 512:1024], sib)
    for k in range(1, 8):
        j = (h + 8 - k) % 8
        arrive(f"x_c{k}", X.at[j, :, 512:1024], sib)

    def product(out, g, col0, width):
        @pl.loop(0, width // 256)
        def _(i):
            rows = X[pl.ds(2 * g, 2)].reshape(256, 1024)
            cols = pl.ds(pl.multiple_of(col0 + i * 256, 256), 256)
            part = jnp.dot(rows, WC[:, cols], preferred_element_type=F32)
            out[:, :, pl.ds(pl.multiple_of(i * 256, 256), 256)] = part.astype(BF).reshape(2, 128, 256)

    groups = [(y + 3) % 4, (y + 1) % 4, (y + 2) % 4, y]
    step_dev = [wdev(0, 1), wdev(0, 3)]
    from_dev = [wdev(0, 3), wdev(0, 1)]
    xdev = wdev(1, 0)
    xo = 1 - xh

    def first(d, s):
        return (y + 3 - s + 4) % 4 if d == 0 else (y + 1 + s) % 4

    def a_piece(d, gi):
        g = groups[gi]
        product(PA.at[d, g], g, d * A_W, A_W)

    def b_piece(d, gi):
        g = groups[gi]
        product(PB.at[d, g], g, 2 * A_W + d * B_W, B_W)
        send(f"bx_{d}{gi}", PB.at[d, g, xo], RBX.at[d, g], xdev)

    a_piece(0, 0)
    send("a_00", PA.at[0, groups[0]], RA.at[0, 0], step_dev[0])
    a_piece(1, 1)
    send("a_10", PA.at[1, groups[1]], RA.at[1, 0], step_dev[1])
    b_piece(0, 0)
    b_piece(1, 1)
    b_piece(0, 2)
    b_piece(1, 2)
    a_piece(0, 2)
    a_piece(1, 2)
    b_piece(0, 1)
    b_piece(1, 0)
    b_piece(0, 3)
    b_piece(1, 3)
    a_piece(0, 1)
    a_piece(1, 0)
    a_piece(0, 3)
    a_piece(1, 3)

    ones = jnp.ones((8, 1024), BF)

    @pl.loop(0, 8)
    def _(b):
        v = X[b].astype(F32)
        SQ[b] = lax.dot_general(
            ones, (v * v).astype(BF), (((1,), (1,)), ((), ())), preferred_element_type=F32
        )

    others = [(dx, dy) for dx in range(2) for dy in range(4) if (dx, dy) != (0, 0)]
    for n, (dx, dy) in enumerate(others):
        b = ((y + dy) % 4) * 2 + (xh + dx) % 2
        send(f"q_{n}", SQ.at[b], SQR.at[n], wdev(dx, dy))

    def add(out, left, right, rows):
        @pl.loop(0, rows // 32)
        def _(i):
            r = pl.ds(pl.multiple_of(i * 32, 32), 32)
            out[r, :] = (left[r, :].astype(F32) + right[r, :].astype(F32)).astype(BF)

    def a_step(s):
        for d in range(2):
            g = first(d, s)
            arrive(f"a_{d}{s - 1}", RA.at[d, s - 1], from_dev[d])
            for e in range(2):
                add(PA.at[d, g, e], PA.at[d, g, e], RA.at[d, s - 1, e], 128)
            if s < 3:
                send(f"a_{d}{s}", PA.at[d, g], RA.at[d, s], step_dev[d])
            else:
                send(f"ax_{d}", PA.at[d, y, xo], RAX.at[d], xdev)

    def b_x(d, gi):
        g = groups[gi]
        arrive(f"bx_{d}{gi}", RBX.at[d, g], xdev)
        add(PB.at[d, g, xh], PB.at[d, g, xh], RBX.at[d, g], 128)

    def b_step(d, s):
        g = first(d, s)
        if s:
            arrive(f"b_{d}{s - 1}", RBY.at[d, s - 1], from_dev[d])
            add(PB.at[d, g, xh], PB.at[d, g, xh], RBY.at[d, s - 1], 128)
        if s < 3:
            send(f"b_{d}{s}", PB.at[d, g, xh], RBY.at[d, s], step_dev[d])

    b_x(0, 0)
    b_step(0, 0)
    b_x(1, 1)
    b_step(1, 0)
    a_step(1)
    b_x(0, 2)
    b_step(0, 1)
    b_x(1, 2)
    b_step(1, 1)
    a_step(2)
    b_x(0, 1)
    b_step(0, 2)
    b_x(1, 0)
    b_step(1, 2)
    b_x(0, 3)
    b_x(1, 3)

    squares = SQ[y * 2 + xh]
    for n, (dx, dy) in enumerate(others):
        arrive(f"q_{n}", SQR.at[n], wdev((2 - dx) % 2, -dy))
        squares = squares + SQR[n]
    scale = lax.rsqrt(jnp.transpose(squares)[:, 0:1] / D + epsilon)

    def gated(left, right, n, col0):
        gate = (left[:, 0:n].astype(F32) + right[:, 0:n].astype(F32)) * scale
        up = (left[:, n : 2 * n].astype(F32) + right[:, n : 2 * n].astype(F32)) * scale
        H[y, xh, :, col0 : col0 + n] = (gate / (1.0 + jnp.exp(-gate)) * up).astype(BF)

    def cols(part, d):
        n = (A_U, B_U)[part]
        o = H_OFF[2 * part + d]
        return slice(o, o + n)

    for d in range(2):
        arrive(f"b_{d}2", RBY.at[d, 2], from_dev[d])
        gated(PB.at[d, y, xh], RBY.at[d, 2], B_U, H_OFF[2 + d])
        piece = H.at[y, xh, :, cols(1, d)]
        send(f"hb_{d}0", piece, piece, step_dev[d])
        send(f"hbx_{d}", piece, piece, xdev)

    def hb_step(s):
        for d in range(2):
            g = first(d, s)
            piece = H.at[g, xh, :, cols(1, d)]
            arrive(f"hb_{d}{s}", piece, from_dev[d])
            if s < 2:
                send(f"hb_{d}{s + 1}", piece, piece, step_dev[d])
            send(f"hbx_{d}{s}", piece, piece, xdev)

    a_step(3)
    hb_step(0)
    hb_step(1)
    hb_step(2)
    for d in range(2):
        arrive(f"ax_{d}", RAX.at[d], xdev)
        gated(PA.at[d, y, xh], RAX.at[d], A_U, H_OFF[d])
        piece = H.at[y, xh, :, cols(0, d)]
        send(f"ha_o{d}0", piece, piece, step_dev[d])
        send(f"hax_{d}", piece, piece, xdev)
    for d in range(2):
        piece = H.at[y, xo, :, cols(0, d)]
        arrive(f"hax_{d}", piece, xdev)
        send(f"ha_p{d}0", piece, piece, step_dev[d])

    loads[2].wait()
    arrive("s_dw", DD.at[1], sib)

    def down(g):
        for e, out in ((0, PDO), (1, PDS)):
            @pl.loop(0, 2)
            def _(i):
                n = pl.ds(pl.multiple_of(i * 256, 256), 256)
                rows = H[g].reshape(256, HALF)
                part = jnp.dot(rows, DD[e, :, n], preferred_element_type=F32)
                out[pl.ds(2 * g, 2), :, n] = part.astype(BF).reshape(2, 128, 256)

    def share(name, g):
        pair = pl.ds(2 * g, 2)
        send(name, PDS.at[pair], PDI.at[pair], sib)

    def ha_step(s):
        for who, e in (("o", xh), ("p", xo)):
            for d in range(2):
                g = first(d, s)
                piece = H.at[g, e, :, cols(0, d)]
                arrive(f"ha_{who}{d}{s}", piece, from_dev[d])
                if s < 2:
                    send(f"ha_{who}{d}{s + 1}", piece, piece, step_dev[d])

    def hb_partner(s):
        for d in range(2):
            g = y if s < 0 else first(d, s)
            arrive(f"hbx_{d}" if s < 0 else f"hbx_{d}{s}", H.at[g, xo, :, cols(1, d)], xdev)

    hb_partner(-1)
    down(y)
    share("d_0", y)
    ha_step(0)
    hb_partner(0)
    ha_step(1)
    hb_partner(1)
    down(groups[2])
    share("d_1", groups[2])
    ha_step(2)
    hb_partner(2)
    down(groups[0])
    share("d_2", groups[0])
    down(groups[1])
    share("d_3", groups[1])

    for n, g in enumerate((y, groups[2], groups[0], groups[1])):
        pair = pl.ds(2 * g, 2)
        arrive(f"d_{n}", PDI.at[pair], sib)
    for k in range(1, 9):
        j = (h + k) % 8
        add(PDO.at[j], PDO.at[j], PDI.at[j], 128)
        if k < 8:
            send(f"f_{k}", PDO.at[j], FR.at[k - 1], hdev(k))
    total = PDO[h].astype(F32)
    for k in range(1, 8):
        arrive(f"f_{k}", FR.at[k - 1], hdev(8 - k))
        total = total + FR[k - 1].astype(F32)
    upd_out[...] = total.astype(BF)

    for cp in sent:
        cp.wait_send()


N_COPIES = 140


def layer(att, gate_up_weight, down_weight, out_weight, residual):
    vm = pltpu.VMEM
    scratch = [
        vm((16, 64, 1024), BF),
        vm((512, 2, HALF), BF),
        vm((512, 2, HALF), BF),
        vm((1024, 2 * HALF), BF),
        vm((2, HALF, 512), BF),
        vm((1024, 512), BF),
        vm((128, 512), BF),
        vm((8, 128, 512), BF),
        vm((7, 128, 512), BF),
        vm((8, 128, 1024), BF),
        vm((2, 4, 2, 128, A_W), BF),
        vm((2, 4, 2, 128, B_W), BF),
        vm((2, 3, 2, 128, A_W), BF),
        vm((2, 128, A_W), BF),
        vm((2, 4, 128, B_W), BF),
        vm((2, 3, 128, B_W), BF),
        vm((8, 8, 128), F32),
        vm((7, 8, 128), F32),
        vm((4, 2, 128, HALF), BF),
        vm((8, 128, 512), BF),
        vm((8, 128, 512), BF),
        vm((8, 128, 512), BF),
        vm((7, 128, 512), BF),
        pltpu.SemaphoreType.DMA((4,)),
        pltpu.SemaphoreType.DMA((N_COPIES,)),
        pltpu.SemaphoreType.DMA((N_COPIES,)),
    ]
    in_vmem = pl.BlockSpec(memory_space=pltpu.VMEM)
    in_hbm = pl.BlockSpec(memory_space=pl.ANY)
    return pl.pallas_call(
        layer_kernel,
        out_shape=(
            jax.ShapeDtypeStruct((128, 512), BF),
            jax.ShapeDtypeStruct((128, 512), BF),
        ),
        in_specs=[in_vmem, in_hbm, in_hbm, in_hbm, in_hbm],
        out_specs=(in_vmem, in_vmem),
        scratch_shapes=scratch,
        name="layer",
        compiler_params=pltpu.CompilerParams(
            collective_id=0, has_side_effects=True, vmem_limit_bytes=60 << 20
        ),
    )(att, gate_up_weight, down_weight, out_weight, residual)


def per_device(
    queries,
    fresh_keys,
    fresh_values,
    cached_keys,
    cached_values,
    context_len,
    tree_size,
    parents,
    residual,
    out_weight,
    gate_up_weight,
    down_weight,
):
    node_count = queries.shape[0]
    kv_local = fresh_keys.shape[1] // HD
    groups = HEADS // KV
    query_heads = queries.reshape(node_count, kv_local, groups, HD)
    cache_k = cached_keys.reshape(-1, kv_local, HD)
    cache_v = cached_values.reshape(-1, kv_local, HD)
    tree_k = fresh_keys.reshape(node_count, kv_local, HD)
    tree_v = fresh_values.reshape(node_count, kv_local, HD)
    attention = attend_request(
        query_heads, cache_k, cache_v, tree_k, tree_v, context_len[0], tree_size[0], parents[0]
    )
    attention_rows = attention.reshape(node_count, kv_local * groups * HD).astype(jnp.bfloat16)
    return layer(attention_rows, gate_up_weight, down_weight, out_weight, residual)


def solution(mesh):
    placed = (
        P("wide", "head"),
        P("wide", "head"),
        P("wide", "head"),
        P("wide", None, "head"),
        P("wide", None, "head"),
        P("wide"),
        P("wide"),
        P("wide", None),
        P(None, "wide"),
        P("head", "wide"),
        P("wide", None, "head"),
        P("head", "wide"),
    )
    return jax.shard_map(
        per_device,
        mesh=mesh,
        in_specs=placed,
        out_specs=(P("head", "wide"), P("head", "wide")),
        check_vma=False,
    )
```

```python
import math

import jax
import jax.numpy as jnp
from jax import lax
from jax.experimental import pallas as pl
from jax.experimental.pallas import tpu as pltpu
from jax.sharding import PartitionSpec as P

D = 8192
HD = 128
CTX = 2048
TREE = 64

epsilon = 1e-05

BF = jnp.bfloat16
F32 = jnp.float32
MESH = pl.DeviceIdType.MESH

A_U = 512
B_U = 384
A_W = 2 * A_U
B_W = 2 * B_U
HALF = 2 * A_U + 2 * B_U
H_OFF = (0, A_U, 2 * A_U, 2 * A_U + B_U)
OTHERS = ((0, 1), (0, 3), (1, 0), (0, 2), (1, 1), (1, 3), (1, 2))

ORDER = (
    "at0", "at1", "u0", "u1", "u2", "gf001", "gf002", "gf003", "gf010", "gf011", "gf012", "gf013",
    "gf103", "gf110", "u3", "gf101", "gf113", "u4", "u5", "gf102", "u6", "gf111", "u7", "gf112",
    "u8", "u9", "u10", "u11", "u12", "u13", "u14", "u15", "op0", "op1", "cm0", "cm1", "xf01",
    "xf02", "xf03", "xf04", "xf05", "xf06", "xf07", "xf11", "xf12", "xr0", "ga00", "xf13", "xf14",
    "xf15", "ga01", "xf16", "xf17", "gb00", "gb01", "xr1", "ga10", "ga11", "as001", "as011",
    "gb10", "gb11", "bs000", "sq0", "sq1", "as101", "bs010", "as111", "as002", "as012", "bs001",
    "bs011", "bs100", "as102", "as112", "bs110", "as003", "as013", "bs002", "bs012", "bs101",
    "sc0", "sc1", "af00", "as113", "as103", "bs111", "af01", "bf00", "hp009", "bf01", "bs102",
    "ho000", "bs112", "af11", "hb000", "ho010", "hp000", "hb010", "af10", "bf10", "bf11", "hp019",
    "ho001", "ho110", "dn00", "hb001", "hp119", "ho011", "hp001", "hb011", "ho100", "hb110",
    "fz00", "hb100", "hp010", "hp109", "ho111", "hb002", "dn10", "hp110", "ho101", "hb012",
    "hb101", "fz10", "hb111", "hp100", "hp011", "dn01", "hb102", "hp111", "hp101", "dn11", "hb112",
    "fz01", "dn02", "fz11", "dn12", "fz02", "fz12", "fo0", "fo1",
)


def layer_kernel(
    queries, fresh_k, fresh_v, parents, length, live, keys_hbm, values_hbm,
    gw, dw, wo_hbm, res_hbm,
    att_out, upd_out,
    KS, VS, FK, FV, S, PR, TB, ATT,
    G, R0, R1, WC, DD, WO, RES, PP, RB, X, PA, PB, RA, RAX, RBX, RBY, SQ, SQR, SC, H, PDO, PDS, PDI, FR,
    lsem, ssem, rsem,
):
    h = lax.axis_index("head")
    w = lax.axis_index("wide")
    xh = w // 8
    y = (w // 2) % 4
    c = w % 2
    flip = 1 - 2 * c
    xo = 1 - xh

    def wide(dxh, dy):
        return (((xh + dxh + 2) % 2) * 4 + (y + dy + 4) % 4) * 2 + c

    sib = (h, w + flip)

    def wdev(dxh, dy):
        return (h, wide(dxh, dy))

    def hdev(k):
        return ((h + k) % 8, w)

    names = {}
    sent = []

    def copy_of(i, src, dst, dev):
        return pltpu.make_async_remote_copy(
            src_ref=src, dst_ref=dst, send_sem=ssem.at[i], recv_sem=rsem.at[i],
            device_id=dev, device_id_type=MESH,
        )

    def send(name, src, dst, dev):
        assert name not in names
        i = names.setdefault(name, len(names))
        cp = copy_of(i, src, dst, dev)
        cp.start()
        sent.append(cp)

    def arrive(name, dst, dev):
        copy_of(names[name], dst, dst, dev).wait_recv()

    mine = pl.ds(pl.multiple_of(c * HALF, 128), HALF)
    other = pl.ds(pl.multiple_of((1 - c) * HALF, 128), HALF)
    loads = [
        pltpu.make_async_copy(keys_hbm.at[0], KS, lsem.at[0]),
        pltpu.make_async_copy(values_hbm.at[0], VS, lsem.at[1]),
        pltpu.make_async_copy(gw.at[:, :, mine], R0, lsem.at[2]),
        pltpu.make_async_copy(wo_hbm, WO, lsem.at[3]),
        pltpu.make_async_copy(
            res_hbm.at[pl.ds(pl.multiple_of(h * 128, 128), 128), :], RES, lsem.at[4]
        ),
        pltpu.make_async_copy(dw.at[mine, :], DD.at[0], lsem.at[5]),
    ]
    for cp in loads:
        cp.start()

    partners = [sib]
    partners += [wdev(dx, dy) for dx, dy in OTHERS]
    partners += [hdev(k) for k in range(1, 8)]
    barrier = pltpu.get_barrier_semaphore()
    for dev in partners:
        pl.semaphore_signal(barrier, inc=1, device_id=dev, device_id_type=MESH)

    node = lax.broadcasted_iota(jnp.int32, (TREE, TREE), 0)
    child = lax.broadcasted_iota(jnp.int32, (TREE, TREE), 1)
    linked = (parents[...] == node) | (node == child)
    reached = jnp.where(linked, 1.0, 0.0).astype(BF)
    for squaring in range(6):
        reached = jnp.minimum(jnp.dot(reached, reached, preferred_element_type=F32), 1.0).astype(BF)
    same = jnp.where(node == child, 1.0, 0.0).astype(BF)
    visible = lax.dot_general(reached, same, (((0,), (0,)), ((), ())), preferred_element_type=F32)
    TB[...] = jnp.full((TREE, 128), -1e30, F32)
    TB[:, 0:TREE] = jnp.where((visible > 0.5) & (child < live[0]), 0.0, -1e30)
    FK[0:TREE] = fresh_k[...]
    FK[TREE:128] = jnp.zeros((128 - TREE, HD), BF)
    FV[0:TREE] = fresh_v[...]
    FV[TREE:128] = jnp.zeros((128 - TREE, HD), BF)
    positions = lax.broadcasted_iota(jnp.int32, (1, CTX), 1)
    cache_bias = jnp.where(positions < length[0], 0.0, -1e30)
    score_scale = 1.0 / math.sqrt(HD)

    def attend(t):
        if t == 0:
            loads[0].wait()
        r0 = 32 * t
        q = jnp.concatenate([queries[r0 : r0 + 32, j * HD : (j + 1) * HD] for j in range(8)], axis=0)
        trans = (((1,), (1,)), ((), ()))

        @pl.loop(0, CTX // 512)
        def _(i):
            n = pl.ds(pl.multiple_of(i * 512, 512), 512)
            S[:, n] = lax.dot_general(q, KS[n, :], trans, preferred_element_type=F32)

        S[:, CTX : CTX + 128] = lax.dot_general(q, FK[...], trans, preferred_element_type=F32)
        if t == 0:
            loads[1].wait()
        tree_bias = TB[r0 : r0 + 32, :]
        alive = lax.broadcasted_iota(jnp.int32, (32, 1), 0) + r0 < live[0]
        denominators = []
        for j in range(8):
            r = slice(32 * j, 32 * j + 32)
            cache = S[r, 0:CTX] * score_scale + cache_bias
            tree = S[r, CTX : CTX + 128] * score_scale + tree_bias
            row_max = jnp.maximum(
                jnp.max(cache, axis=1, keepdims=True), jnp.max(tree, axis=1, keepdims=True)
            )
            cache = jnp.exp(cache - row_max)
            tree = jnp.exp(tree - row_max)
            denominators.append(
                jnp.sum(cache, axis=1, keepdims=True) + jnp.sum(tree, axis=1, keepdims=True)
            )
            PR[r, 0:CTX] = cache.astype(BF)
            PR[r, CTX : CTX + 128] = tree.astype(BF)
        out = jnp.dot(PR[:, 0:CTX], VS[...], preferred_element_type=F32)
        out = out + jnp.dot(PR[:, CTX : CTX + 128], FV[...], preferred_element_type=F32)
        for j in range(8):
            part = out[32 * j : 32 * j + 32] / denominators[j]
            ATT[t, :, j * HD : (j + 1) * HD] = jnp.where(alive, part, 0.0).astype(BF)
        if t == 0:
            pl.semaphore_wait(barrier, len(partners))
        for dx, dy in OTHERS:
            send(f"g{t}{dx}{dy}", ATT.at[t], G.at[t, w], wdev(dx, dy))
        send(f"gc{t}", ATT.at[t], G.at[t, w], sib)
        if t == 0:
            send("s_gw", gw.at[:, :, other], R1, sib)
            send("s_dw", dw.at[other, :], DD.at[1], sib)
        G[t, w] = ATT[t]

    def gather_on(t, dx, dy):
        src = wide(-dx, -dy)
        arrive(f"g{t}{dx}{dy}", G.at[t, src], wdev(-dx, -dy))
        send(f"gc{t}{dx}{dy}", G.at[t, src], G.at[t, src], sib)

    def untwist(k):
        if k == 0:
            loads[2].wait()
        if k == 8:
            arrive("s_gw", R1, sib)
        raw = R0 if k < 8 else R1
        i = k % 8
        b = raw[64 * i : 64 * i + 64]
        gate, up = b[:, 0, :], b[:, 1, :]
        o = slice(64 * k, 64 * k + 64)
        for p in range(4):
            n = A_U if p < 2 else B_U
            u = H_OFF[p]
            WC[o, 2 * u : 2 * u + n] = gate[:, u : u + n]
            WC[o, 2 * u + n : 2 * u + 2 * n] = up[:, u : u + n]

    def project(t):
        arrive(f"gc{t}", G.at[t, w + flip], sib)
        for dx, dy in OTHERS:
            arrive(f"gc{t}{dx}{dy}", G.at[t, wide(-dx, -dy) + flip], sib)
        if t == 0:
            loads[3].wait()
        rows = G[t].reshape(512, 1024)
        PP[t] = jnp.dot(rows, WO[...], preferred_element_type=F32).astype(BF).reshape(8, 64, 512)
        for k in range(1, 8):
            send(f"o{t}{k}", PP.at[t, (h + k) % 8], RB.at[t, k - 1], hdev(k))

    def combine(t):
        if t == 0:
            loads[4].wait()
        rows = (slice(32 * t, 32 * t + 32), slice(64 + 32 * t, 96 + 32 * t))
        total = PP[t, h].astype(F32) + jnp.concatenate([RES[r, :] for r in rows], axis=0).astype(F32)
        for k in range(1, 8):
            arrive(f"o{t}{k}", RB.at[t, k - 1], hdev(8 - k))
            total = total + RB[t, k - 1].astype(F32)
        rounded = total.astype(BF)
        X[t, h, :, 0:512] = rounded
        own = X.at[t, h, :, 0:512]
        for k in range(1, 8):
            send(f"x{t}{k}", own, own, hdev(k))
        send(f"xc{t}", own, X.at[t, h, :, 512:1024], sib)
        att_out[rows[0], :] = rounded[0:32]
        att_out[rows[1], :] = rounded[32:64]

    def spread(t, k):
        j = (h + 8 - k) % 8
        arrive(f"x{t}{k}", X.at[t, j, :, 0:512], hdev(8 - k))
        send(f"xc{t}{k}", X.at[t, j, :, 0:512], X.at[t, j, :, 512:1024], sib)

    def spread_end(t):
        arrive(f"xc{t}", X.at[t, h, :, 512:1024], sib)
        for k in range(1, 8):
            arrive(f"xc{t}{k}", X.at[t, (h + 8 - k) % 8, :, 512:1024], sib)

    step_dev = [wdev(0, 1), wdev(0, 3)]
    from_dev = [wdev(0, 3), wdev(0, 1)]
    xdev = wdev(1, 0)

    def first(d, s):
        return (y + 3 - s + 4) % 4 if d == 0 else (y + 1 + s) % 4

    def product(t, out, col0, width):
        @pl.loop(0, width // 256)
        def _(i):
            rows = X[t].reshape(512, 1024)
            cols = pl.ds(pl.multiple_of(col0 + i * 256, 256), 256)
            part = jnp.dot(rows, WC[:, cols], preferred_element_type=F32).astype(BF)
            out[:, :, :, pl.ds(pl.multiple_of(i * 256, 256), 256)] = part.reshape(4, 2, 64, 256)

    def a_piece(t, d):
        product(t, PA.at[t, d], d * A_W, A_W)
        send(f"a{t}{d}0", PA.at[t, d, first(d, 0)], RA.at[t, d, 0], step_dev[d])

    def b_piece(t, d):
        product(t, PB.at[t, d], 2 * A_W + d * B_W, B_W)
        for s in range(4):
            g = first(d, s)
            send(f"bx{t}{d}{s}", PB.at[t, d, g, xo], RBX.at[t, d, s], xdev)

    def squares(t):
        ones = jnp.ones((8, 1024), BF)
        for b in range(8):
            v = X[t, b].astype(F32)
            part = lax.dot_general(
                ones, (v * v).astype(BF), (((1,), (1,)), ((), ())), preferred_element_type=F32
            )
            SQ[t, b] = jnp.concatenate([part, part], axis=1)
        for n, (dx, dy) in enumerate(OTHERS):
            b = ((y + dy) % 4) * 2 + (xh + dx) % 2
            send(f"q{t}{n}", SQ.at[t, b], SQR.at[t, n], wdev(dx, dy))

    def row_scale(t):
        total = SQ[t, y * 2 + xh]
        for n, (dx, dy) in enumerate(OTHERS):
            arrive(f"q{t}{n}", SQR.at[t, n], wdev(-dx, -dy))
            total = total + SQR[t, n]
        scale = lax.rsqrt(jnp.transpose(total)[0:64, 0:1] / D + epsilon)
        SC[t] = jnp.broadcast_to(scale, (64, 128))

    def add(out, left, right):
        for i in range(2):
            r = slice(32 * i, 32 * i + 32)
            out[r, :] = (left[r, :].astype(F32) + right[r, :].astype(F32)).astype(BF)

    def a_step(t, d, s):
        g = first(d, s)
        arrive(f"a{t}{d}{s - 1}", RA.at[t, d, s - 1], from_dev[d])
        for e in range(2):
            add(PA.at[t, d, g, e], PA.at[t, d, g, e], RA.at[t, d, s - 1, e])
        if s < 3:
            send(f"a{t}{d}{s}", PA.at[t, d, g], RA.at[t, d, s], step_dev[d])
        else:
            send(f"xx{t}{d}", PA.at[t, d, y, xo], RAX.at[t, d], xdev)

    def b_sum(t, d, s):
        g = first(d, s)
        out = PB.at[t, d, g, xh]
        arrive(f"bx{t}{d}{s}", RBX.at[t, d, s], xdev)
        add(out, out, RBX.at[t, d, s])
        if s and s < 3:
            arrive(f"b{t}{d}{s - 1}", RBY.at[t, d, s - 1], from_dev[d])
            add(out, out, RBY.at[t, d, s - 1])
        if s < 3:
            send(f"b{t}{d}{s}", out, RBY.at[t, d, s], step_dev[d])

    def gated(t, left, right, n, col0):
        scale = SC[t, :, 0:1]
        gate = (left[:, 0:n].astype(F32) + right[:, 0:n].astype(F32)) * scale
        up = (left[:, n : 2 * n].astype(F32) + right[:, n : 2 * n].astype(F32)) * scale
        H[t, y, xh, :, col0 : col0 + n] = (gate / (1.0 + jnp.exp(-gate)) * up).astype(BF)

    def cols(part, d):
        o = H_OFF[2 * part + d]
        return slice(o, o + (A_U, B_U)[part])

    def b_end(t, d):
        b_sum(t, d, 3)
        arrive(f"b{t}{d}2", RBY.at[t, d, 2], from_dev[d])
        gated(t, PB.at[t, d, y, xh], RBY.at[t, d, 2], B_U, H_OFF[2 + d])
        piece = H.at[t, y, xh, :, cols(1, d)]
        send(f"hb{t}{d}0", piece, piece, step_dev[d])
        send(f"hx{t}{d}9", piece, piece, xdev)

    def hb_step(t, d, s):
        piece = H.at[t, first(d, s), xh, :, cols(1, d)]
        arrive(f"hb{t}{d}{s}", piece, from_dev[d])
        if s < 2:
            send(f"hb{t}{d}{s + 1}", piece, piece, step_dev[d])
        send(f"hx{t}{d}{s}", piece, piece, xdev)

    def a_end(t, d):
        arrive(f"xx{t}{d}", RAX.at[t, d], xdev)
        gated(t, PA.at[t, d, y, xh], RAX.at[t, d], A_U, H_OFF[d])
        piece = H.at[t, y, xh, :, cols(0, d)]
        send(f"ho{t}{d}0", piece, piece, step_dev[d])
        send(f"hp{t}{d}9", piece, piece, xdev)

    def ha_step(t, d, s, q):
        if s == 9:
            piece = H.at[t, y, xo, :, cols(0, d)]
            arrive(f"hp{t}{d}9", piece, xdev)
            send(f"hp{t}{d}0", piece, piece, step_dev[d])
            return
        piece = H.at[t, first(d, s), xh if q == "o" else xo, :, cols(0, d)]
        arrive(f"h{q}{t}{d}{s}", piece, from_dev[d])
        if s < 2:
            send(f"h{q}{t}{d}{s + 1}", piece, piece, step_dev[d])

    down_ready = []

    def down(t, i):
        if not down_ready:
            loads[5].wait()
            arrive("s_dw", DD.at[1], sib)
            down_ready.append(True)
        steps = ((9,), (1,), (0, 2))[i]
        for s in steps:
            for d in range(2):
                g = y if s == 9 else first(d, s)
                arrive(f"hx{t}{d}{s}", H.at[t, g, xo, :, cols(1, d)], xdev)
                if s == 2:
                    ha_step(t, d, 2, "o")
                    ha_step(t, d, 2, "p")
        gs = ((y,), ((y + 2) % 4,), ((y + 1) % 4, (y + 3) % 4))[i]
        for e, out in ((1, PDS), (0, PDO)):
            @pl.loop(0, 2)
            def _(n):
                n = pl.ds(pl.multiple_of(n * 256, 256), 256)
                rows = jnp.concatenate([H[t, g].reshape(128, HALF) for g in gs], axis=0)
                part = jnp.dot(rows, DD[e, :, n], preferred_element_type=F32).astype(BF)
                for m, g in enumerate(gs):
                    out[t, pl.ds(2 * g, 2), :, n] = part[128 * m : 128 * m + 128].reshape(2, 64, 256)

            if e:
                for m, g in enumerate(gs):
                    pair = pl.ds(2 * g, 2)
                    send(f"sh{t}{i}{m}", PDS.at[t, pair], PDI.at[t, pair], sib)

    def share(t, i):
        gs = ((y,), ((y + 2) % 4,), ((y + 1) % 4, (y + 3) % 4))[i]
        for k in range(1, 8):
            names.setdefault(f"f{t}{k}", len(names))
        base = names[f"f{t}1"]
        for m, g in enumerate(gs):
            pair = pl.ds(2 * g, 2)
            arrive(f"sh{t}{i}{m}", PDI.at[t, pair], sib)
            for e in range(2):
                j = 2 * g + e
                k = (j - h + 8) % 8
                add(PDO.at[t, j], PDO.at[t, j], PDI.at[t, j])

                @pl.when(k != 0)
                def _():
                    copy_of(base + k - 1, PDO.at[t, j], FR.at[t, k - 1], (j, w)).start()

    def finish(t):
        total = PDO[t, h].astype(F32)
        for k in range(1, 8):
            arrive(f"f{t}{k}", FR.at[t, k - 1], hdev(8 - k))
            total = total + FR[t, k - 1].astype(F32)
            sent.append(copy_of(names[f"f{t}{k}"], PDO.at[t, (h + k) % 8], FR.at[t, k - 1], hdev(k)))
        rounded = total.astype(BF)
        upd_out[32 * t : 32 * t + 32, :] = rounded[0:32]
        upd_out[64 + 32 * t : 96 + 32 * t, :] = rounded[32:64]

    steps = {}
    for k in range(16):
        steps[f"u{k}"] = (untwist, k)
    for t in range(2):
        steps[f"at{t}"] = (attend, t)
        for dx, dy in OTHERS:
            steps[f"gf{t}{dx}{dy}"] = (gather_on, t, dx, dy)
        steps[f"op{t}"] = (project, t)
        steps[f"cm{t}"] = (combine, t)
        for k in range(1, 8):
            steps[f"xf{t}{k}"] = (spread, t, k)
        steps[f"xr{t}"] = (spread_end, t)
        steps[f"sq{t}"] = (squares, t)
        steps[f"sc{t}"] = (row_scale, t)
        for d in range(2):
            steps[f"ga{t}{d}"] = (a_piece, t, d)
            steps[f"gb{t}{d}"] = (b_piece, t, d)
            for s in range(3):
                steps[f"as{t}{d}{s + 1}"] = (a_step, t, d, s + 1)
                steps[f"bs{t}{d}{s}"] = (b_sum, t, d, s)
                steps[f"hb{t}{d}{s}"] = (hb_step, t, d, s)
            steps[f"bf{t}{d}"] = (b_end, t, d)
            steps[f"af{t}{d}"] = (a_end, t, d)
            for s in (0, 1):
                for q in "op":
                    steps[f"h{q}{t}{d}{s}"] = (ha_step, t, d, s, q)
            steps[f"hp{t}{d}9"] = (ha_step, t, d, 9, "p")
        for i in range(3):
            steps[f"dn{t}{i}"] = (down, t, i)
            steps[f"fz{t}{i}"] = (share, t, i)
        steps[f"fo{t}"] = (finish, t)
    assert sorted(steps) == sorted(ORDER)
    for name in ORDER:
        step, *where = steps[name]
        step(*where)

    assert len(names) <= N_COPIES
    for cp in sent:
        cp.wait_send()


N_COPIES = 232


def layer(
    queries, fresh_keys, fresh_values, cached_keys, cached_values, context_len, tree_size, parents,
    residual, out_weight, gate_up_weight, down_weight,
):
    vm = pltpu.VMEM
    scratch = [
        vm((CTX, HD), BF),
        vm((CTX, HD), BF),
        vm((128, HD), BF),
        vm((128, HD), BF),
        vm((256, CTX + 128), F32),
        vm((256, CTX + 128), BF),
        vm((TREE, 128), F32),
        vm((2, 32, 1024), BF),
        vm((2, 16, 32, 1024), BF),
        vm((512, 2, HALF), BF),
        vm((512, 2, HALF), BF),
        vm((1024, 2 * HALF), BF),
        vm((2, HALF, 512), BF),
        vm((1024, 512), BF),
        vm((128, 512), BF),
        vm((2, 8, 64, 512), BF),
        vm((2, 7, 64, 512), BF),
        vm((2, 8, 64, 1024), BF),
        vm((2, 2, 4, 2, 64, A_W), BF),
        vm((2, 2, 4, 2, 64, B_W), BF),
        vm((2, 2, 3, 2, 64, A_W), BF),
        vm((2, 2, 64, A_W), BF),
        vm((2, 2, 4, 64, B_W), BF),
        vm((2, 2, 3, 64, B_W), BF),
        vm((2, 8, 8, 128), F32),
        vm((2, 7, 8, 128), F32),
        vm((2, 64, 128), F32),
        vm((2, 4, 2, 64, HALF), BF),
        vm((2, 8, 64, 512), BF),
        vm((2, 8, 64, 512), BF),
        vm((2, 8, 64, 512), BF),
        vm((2, 7, 64, 512), BF),
        pltpu.SemaphoreType.DMA((6,)),
        pltpu.SemaphoreType.DMA((N_COPIES,)),
        pltpu.SemaphoreType.DMA((N_COPIES,)),
    ]
    in_vmem = pl.BlockSpec(memory_space=pltpu.VMEM)
    in_smem = pl.BlockSpec(memory_space=pltpu.SMEM)
    in_hbm = pl.BlockSpec(memory_space=pl.ANY)
    return pl.pallas_call(
        layer_kernel,
        out_shape=(
            jax.ShapeDtypeStruct((128, 512), BF),
            jax.ShapeDtypeStruct((128, 512), BF),
        ),
        in_specs=[in_vmem] * 4 + [in_smem] * 2 + [in_hbm] * 6,
        out_specs=(in_vmem, in_vmem),
        scratch_shapes=scratch,
        name="layer",
        compiler_params=pltpu.CompilerParams(
            collective_id=0, has_side_effects=True, vmem_limit_bytes=60 << 20
        ),
    )(
        queries, fresh_keys, fresh_values, parents, context_len, tree_size, cached_keys, cached_values,
        gate_up_weight, down_weight, out_weight, residual,
    )


def solution(mesh):
    placed = (
        P("wide", "head"),
        P("wide", "head"),
        P("wide", "head"),
        P("wide", None, "head"),
        P("wide", None, "head"),
        P("wide"),
        P("wide"),
        P("wide", None),
        P(None, "wide"),
        P("head", "wide"),
        P("wide", None, "head"),
        P("head", "wide"),
    )
    return jax.shard_map(
        layer,
        mesh=mesh,
        in_specs=placed,
        out_specs=(P("head", "wide"), P("head", "wide")),
        check_vma=False,
    )
```

```python
import math

import jax
import jax.numpy as jnp
from jax import lax
from jax.experimental import pallas as pl
from jax.experimental.pallas import tpu as pltpu
from jax.sharding import PartitionSpec as P

D = 8192
HD = 128
CTX = 2048
TREE = 64

epsilon = 1e-05

BF = jnp.bfloat16
F32 = jnp.float32
MESH = pl.DeviceIdType.MESH

A_U = 512
B_U = 384
A_W = 2 * A_U
B_W = 2 * B_U
HALF = 2 * A_U + 2 * B_U
H_OFF = (0, A_U, 2 * A_U, 2 * A_U + B_U)
OTHERS = ((0, 1), (0, 3), (1, 0), (0, 2), (1, 1), (1, 3), (1, 2))

ORDER = (
    "in", "at0", "at1", "u0", "u1", "u2", "gf003", "gf001", "u3", "u4", "gf002", "gf011", "gf012",
    "gf013", "gf010", "u5", "gf103", "u6", "op0", "gf111", "gf101", "gf110", "gf102", "gf113",
    "u7", "gf112", "u8", "u9", "op1", "u10", "u11", "u12", "cm0", "u13", "u14", "u15", "cm1",
    "xf01", "xf03", "xf02", "xf04", "xf05", "xf07", "xf06", "xf11", "xr0", "ga00", "xf13", "xf15",
    "xf12", "ga01", "gb01", "gb00", "xf17", "xf16", "xf14", "sq0", "as001", "bs010", "xr1", "ga11",
    "as011", "ga10", "bs011", "gb11", "gb10", "as002", "sq1", "bs000", "as111", "as101", "sc0",
    "as012", "bs110", "bs012", "as003", "bs001", "as112", "bs100", "as102", "bs002", "as013",
    "bs101", "bs111", "sc1", "bf01", "af00", "as103", "af01", "bf00", "as113", "hp009", "bs102",
    "bs112", "hb010", "ho000", "hb000", "af10", "ho010", "hp000", "hp019", "bf11", "dn00", "bf10",
    "ho011", "hb011", "ho001", "af11", "hb001", "hp010", "fz00", "hb110", "ho100", "hp001",
    "hp109", "hb012", "hb100", "ho110", "hb002", "hp011", "hp119", "dn10", "hb111", "ho101",
    "ho111", "dn01", "hp100", "fz10", "hb101", "hp110", "fz01", "dn02", "hb112", "hp101", "hb102",
    "hp111", "dn11", "fz02", "dn12", "fz11", "fx0", "fz12", "fo0", "fx1", "fo1",
)


def layer_kernel(
    queries, fresh_k, fresh_v, parents, length, live, keys_hbm, values_hbm,
    gw, dw, wo_hbm, res_hbm,
    out,
    KS, VS, FK, FV, S, PR, TB, ATT,
    G, R0, R1, WC, DD, WO, RES, PP, RB, X, PA, PB, RA, RAX, RBX, RBY, SQ, SQR, SC, H, PDO, PDS, PDI, FR, FS, FXR,
    lsem, ssem, rsem,
):
    h = lax.axis_index("head")
    w = lax.axis_index("wide")
    xh = w // 8
    y = (w // 2) % 4
    c = w % 2
    flip = 1 - 2 * c
    xo = 1 - xh

    def wide(dxh, dy):
        return (((xh + dxh + 2) % 2) * 4 + (y + dy + 4) % 4) * 2 + c

    sib = (h, w + flip)
    xl = h // 4
    z = h % 4

    def place(j):
        return 2 * (j % 4) + j // 4

    def wdev(dxh, dy):
        return (h, wide(dxh, dy))

    def hdev(k):
        return ((h + k) % 8, w)

    names = {}
    sent = []

    def copy_of(i, src, dst, dev):
        return pltpu.make_async_remote_copy(
            src_ref=src, dst_ref=dst, send_sem=ssem.at[0], recv_sem=rsem.at[i],
            device_id=dev, device_id_type=MESH,
        )

    def send(name, src, dst, dev):
        i = names.setdefault(name, len(names))
        cp = copy_of(i, src, dst, dev)
        cp.start()
        sent.append(cp)

    def arrive(name, dst, dev):
        copy_of(names[name], dst, dst, dev).wait_recv()

    mine = pl.ds(pl.multiple_of(c * HALF, 128), HALF)
    other = pl.ds(pl.multiple_of((1 - c) * HALF, 128), HALF)
    loads = [
        pltpu.make_async_copy(keys_hbm.at[0], KS, lsem.at[0]),
        pltpu.make_async_copy(values_hbm.at[0], VS, lsem.at[1]),
        pltpu.make_async_copy(gw.at[:, :, mine], R0, lsem.at[2]),
        pltpu.make_async_copy(wo_hbm, WO, lsem.at[3]),
        pltpu.make_async_copy(
            res_hbm.at[pl.ds(pl.multiple_of(h * 128, 128), 128), :], RES, lsem.at[4]
        ),
        pltpu.make_async_copy(dw.at[mine, :], DD.at[0], lsem.at[5]),
    ]
    for cp in loads:
        cp.start()

    partners = [sib]
    partners += [wdev(dx, dy) for dx, dy in OTHERS]
    partners += [hdev(k) for k in range(1, 8)]
    barrier = pltpu.get_barrier_semaphore()
    for dev in partners:
        pl.semaphore_signal(barrier, inc=1, device_id=dev, device_id_type=MESH)

    def enter():
        pl.semaphore_wait(barrier, len(partners))
        send("s_gw", gw.at[:, :, other], R1, sib)

    node = lax.broadcasted_iota(jnp.int32, (TREE, TREE), 0)
    child = lax.broadcasted_iota(jnp.int32, (TREE, TREE), 1)
    linked = (parents[...] == node) | (node == child)
    reached = jnp.where(linked, 1.0, 0.0).astype(BF)
    for squaring in range(6):
        reached = jnp.minimum(jnp.dot(reached, reached, preferred_element_type=F32), 1.0).astype(BF)
    same = jnp.where(node == child, 1.0, 0.0).astype(BF)
    visible = lax.dot_general(reached, same, (((0,), (0,)), ((), ())), preferred_element_type=F32)
    TB[...] = jnp.full((TREE, 128), -1e30, F32)
    TB[:, 0:TREE] = jnp.where((visible > 0.5) & (child < live[0]), 0.0, -1e30)
    FK[0:TREE] = fresh_k[...]
    FK[TREE:128] = jnp.zeros((128 - TREE, HD), BF)
    FV[0:TREE] = fresh_v[...]
    FV[TREE:128] = jnp.zeros((128 - TREE, HD), BF)
    positions = lax.broadcasted_iota(jnp.int32, (1, CTX), 1)
    cache_bias = jnp.where(positions < length[0], 0.0, -1e30)
    score_scale = math.log2(math.e) / math.sqrt(HD)

    def attend(t):
        if t == 0:
            loads[0].wait()
        r0 = 32 * t
        q = jnp.concatenate([queries[r0 : r0 + 32, j * HD : (j + 1) * HD] for j in range(8)], axis=0)
        trans = (((1,), (1,)), ((), ()))

        @pl.loop(0, CTX // 512)
        def _(i):
            n = pl.ds(pl.multiple_of(i * 512, 512), 512)
            S[:, n] = lax.dot_general(q, KS[n, :], trans, preferred_element_type=F32)

        S[:, CTX : CTX + 128] = lax.dot_general(q, FK[...], trans, preferred_element_type=F32)
        if t == 0:
            loads[1].wait()
        alive = lax.broadcasted_iota(jnp.int32, (32, 1), 0) + r0 < live[0]
        denominators = []
        for j in range(16):
            r = slice(16 * j, 16 * j + 16)
            n0 = r0 + 16 * (j % 2)
            cache = S[r, 0:CTX] + cache_bias
            tree = S[r, CTX : CTX + 128] + TB[n0 : n0 + 16, :]
            row_max = jnp.maximum(
                jnp.max(cache, axis=1, keepdims=True), jnp.max(tree, axis=1, keepdims=True)
            )
            cache = jnp.exp2((cache - row_max) * score_scale)
            tree = jnp.exp2((tree - row_max) * score_scale)
            denominators.append(
                jnp.sum(cache, axis=1, keepdims=True) + jnp.sum(tree, axis=1, keepdims=True)
            )
            PR[r, 0:CTX] = cache.astype(BF)
            PR[r, CTX : CTX + 128] = tree.astype(BF)
        mixed = jnp.dot(PR[:, 0:CTX], VS[...], preferred_element_type=F32)
        mixed = mixed + jnp.dot(PR[:, CTX : CTX + 128], FV[...], preferred_element_type=F32)
        for j in range(8):
            below = jnp.concatenate(denominators[2 * j : 2 * j + 2], axis=0)
            part = mixed[32 * j : 32 * j + 32] / below
            ATT[t, :, j * HD : (j + 1) * HD] = jnp.where(alive, part, 0.0).astype(BF)
        for dx, dy in OTHERS:
            send(f"g{t}{dx}{dy}", ATT.at[t], G.at[t, w], wdev(dx, dy))
        send(f"gc{t}", ATT.at[t], G.at[t, w], sib)
        G[t, w] = ATT[t]

    def gather_on(t, dx, dy):
        src = wide(-dx, -dy)
        arrive(f"g{t}{dx}{dy}", G.at[t, src], wdev(-dx, -dy))
        send(f"gc{t}", G.at[t, src], G.at[t, src], sib)

    def untwist(k):
        if k == 0:
            loads[2].wait()
        if k == 8:
            arrive("s_gw", R1, sib)
        raw = R0 if k < 8 else R1
        i = k % 8
        b = raw[64 * i : 64 * i + 64]
        gate, up = b[:, 0, :], b[:, 1, :]
        o = slice(64 * k, 64 * k + 64)
        for p in range(4):
            n = A_U if p < 2 else B_U
            u = H_OFF[p]
            WC[o, 2 * u : 2 * u + n] = gate[:, u : u + n]
            WC[o, 2 * u + n : 2 * u + 2 * n] = up[:, u : u + n]

    def project(t):
        arrive(f"gc{t}", G.at[t, 0:8], sib)
        if t == 0:
            loads[3].wait()
        rows = G[t].reshape(512, 1024)
        PP[t] = jnp.dot(rows, WO[...], preferred_element_type=F32).astype(BF).reshape(8, 64, 512)
        if t == 1:
            send("s_dw", dw.at[other, :], DD.at[1], sib)
        for k in range(1, 8):
            send(f"o{t}", PP.at[t, (h + k) % 8], RB.at[t, k - 1], hdev(k))

    def combine(t):
        if t == 0:
            loads[4].wait()
        rows = (slice(32 * t, 32 * t + 32), slice(64 + 32 * t, 96 + 32 * t))
        total = PP[t, h].astype(F32) + jnp.concatenate([RES[r, :] for r in rows], axis=0).astype(F32)
        arrive(f"o{t}", RB.at[t], hdev(1))
        for k in range(7):
            total = total + RB[t, k].astype(F32)
        rounded = total.astype(BF)
        own = X.at[t, place(h), :, 0:512]
        own[...] = rounded
        for k in range(1, 8):
            send(f"x{t}{k}", own, own, hdev(k))
        send(f"xc{t}", own, X.at[t, place(h), :, 512:1024], sib)
        out[0, rows[0], :] = rounded[0:32]
        out[0, rows[1], :] = rounded[32:64]

    def spread(t, k):
        j = place((h + 8 - k) % 8)
        arrive(f"x{t}{k}", X.at[t, j, :, 0:512], hdev(8 - k))
        send(f"xc{t}", X.at[t, j, :, 0:512], X.at[t, j, :, 512:1024], sib)

    def spread_end(t):
        arrive(f"xc{t}", X.at[t, :, :, 512:1024], sib)

    step_dev = [wdev(0, 1), wdev(0, 3)]
    from_dev = [wdev(0, 3), wdev(0, 1)]
    xdev = wdev(1, 0)

    def first(d, s):
        return (y + 3 - s + 4) % 4 if d == 0 else (y + 1 + s) % 4

    def product(t, out, col0, width):
        @pl.loop(0, width // 256)
        def _(i):
            rows = X[t].reshape(512, 1024)
            cols = pl.ds(pl.multiple_of(col0 + i * 256, 256), 256)
            part = jnp.dot(rows, WC[:, cols], preferred_element_type=F32).astype(BF)
            out[:, :, :, pl.ds(pl.multiple_of(i * 256, 256), 256)] = part.reshape(4, 2, 64, 256)

    def a_piece(t, d):
        product(t, PA.at[t, d], d * A_W, A_W)
        send(f"a{t}{d}0", PA.at[t, d, first(d, 0)], RA.at[t, d, 0], step_dev[d])

    def b_piece(t, d):
        product(t, PB.at[t, d], 2 * A_W + d * B_W, B_W)
        for s in range(4):
            g = first(d, s)
            send(f"bx{t}{d}{s}", PB.at[t, d, g, xo], RBX.at[t, d, s], xdev)

    def squares(t):
        ones = jnp.ones((8, 1024), BF)
        for b in range(8):
            v = X[t, b].astype(F32)
            part = lax.dot_general(
                ones, (v * v).astype(BF), (((1,), (1,)), ((), ())), preferred_element_type=F32
            )
            SQ[t, b] = jnp.concatenate([part, part], axis=1)
        for n, (dx, dy) in enumerate(OTHERS):
            b = ((y + dy) % 4) * 2 + (xh + dx) % 2
            send(f"q{t}", SQ.at[t, b], SQR.at[t, n], wdev(dx, dy))

    def row_scale(t):
        total = SQ[t, y * 2 + xh]
        arrive(f"q{t}", SQR.at[t], wdev(0, 1))
        for n in range(7):
            total = total + SQR[t, n]
        scale = lax.rsqrt(jnp.transpose(total)[0:64, 0:1] / D + epsilon)
        SC[t] = jnp.broadcast_to(scale, (64, 128))

    def add(out, left, right):
        for i in range(2):
            r = slice(32 * i, 32 * i + 32)
            out[r, :] = (left[r, :].astype(F32) + right[r, :].astype(F32)).astype(BF)

    def a_step(t, d, s):
        g = first(d, s)
        arrive(f"a{t}{d}{s - 1}", RA.at[t, d, s - 1], from_dev[d])
        for e in range(2):
            add(PA.at[t, d, g, e], PA.at[t, d, g, e], RA.at[t, d, s - 1, e])
        if s < 3:
            send(f"a{t}{d}{s}", PA.at[t, d, g], RA.at[t, d, s], step_dev[d])
        else:
            send(f"xx{t}{d}", PA.at[t, d, y, xo], RAX.at[t, d], xdev)

    def b_sum(t, d, s):
        g = first(d, s)
        out = PB.at[t, d, g, xh]
        arrive(f"bx{t}{d}{s}", RBX.at[t, d, s], xdev)
        add(out, out, RBX.at[t, d, s])
        if s and s < 3:
            arrive(f"b{t}{d}{s - 1}", RBY.at[t, d, s - 1], from_dev[d])
            add(out, out, RBY.at[t, d, s - 1])
        if s < 3:
            send(f"b{t}{d}{s}", out, RBY.at[t, d, s], step_dev[d])

    def gated(t, left, right, n, col0):
        scale = SC[t, :, 0:1]
        gate = (left[:, 0:n].astype(F32) + right[:, 0:n].astype(F32)) * scale
        up = (left[:, n : 2 * n].astype(F32) + right[:, n : 2 * n].astype(F32)) * scale
        H[t, y, xh, :, col0 : col0 + n] = (gate / (1.0 + jnp.exp(-gate)) * up).astype(BF)

    def cols(part, d):
        o = H_OFF[2 * part + d]
        return slice(o, o + (A_U, B_U)[part])

    def b_end(t, d):
        b_sum(t, d, 3)
        arrive(f"b{t}{d}2", RBY.at[t, d, 2], from_dev[d])
        gated(t, PB.at[t, d, y, xh], RBY.at[t, d, 2], B_U, H_OFF[2 + d])
        piece = H.at[t, y, xh, :, cols(1, d)]
        send(f"hb{t}{d}0", piece, piece, step_dev[d])
        send(f"hx{t}{d}9", piece, piece, xdev)

    def hb_step(t, d, s):
        piece = H.at[t, first(d, s), xh, :, cols(1, d)]
        arrive(f"hb{t}{d}{s}", piece, from_dev[d])
        if s < 2:
            send(f"hb{t}{d}{s + 1}", piece, piece, step_dev[d])
        send(f"hx{t}{d}{s}", piece, piece, xdev)

    def a_end(t, d):
        arrive(f"xx{t}{d}", RAX.at[t, d], xdev)
        gated(t, PA.at[t, d, y, xh], RAX.at[t, d], A_U, H_OFF[d])
        piece = H.at[t, y, xh, :, cols(0, d)]
        send(f"ho{t}{d}0", piece, piece, step_dev[d])
        send(f"hp{t}{d}9", piece, piece, xdev)

    def ha_step(t, d, s, q):
        if s == 9:
            piece = H.at[t, y, xo, :, cols(0, d)]
            arrive(f"hp{t}{d}9", piece, xdev)
            send(f"hp{t}{d}0", piece, piece, step_dev[d])
            return
        piece = H.at[t, first(d, s), xh if q == "o" else xo, :, cols(0, d)]
        arrive(f"h{q}{t}{d}{s}", piece, from_dev[d])
        if s < 2:
            send(f"h{q}{t}{d}{s + 1}", piece, piece, step_dev[d])

    down_ready = []

    def down(t, i):
        if not down_ready:
            loads[5].wait()
            arrive("s_dw", DD.at[1], sib)
            down_ready.append(True)
        steps = ((9,), (1,), (0, 2))[i]
        for s in steps:
            for d in range(2):
                g = y if s == 9 else first(d, s)
                arrive(f"hx{t}{d}{s}", H.at[t, g, xo, :, cols(1, d)], xdev)
                if s == 2:
                    ha_step(t, d, 2, "o")
                    ha_step(t, d, 2, "p")
        gs = ((y,), ((y + 2) % 4,), ((y + 1) % 4, (y + 3) % 4))[i]
        for e, out in ((1, PDS), (0, PDO)):
            @pl.loop(0, 2)
            def _(n):
                n = pl.ds(pl.multiple_of(n * 256, 256), 256)
                rows = jnp.concatenate([H[t, g].reshape(128, HALF) for g in gs], axis=0)
                part = jnp.dot(rows, DD[e, :, n], preferred_element_type=F32).astype(BF)
                for m, g in enumerate(gs):
                    out[t, pl.ds(2 * g, 2), :, n] = part[128 * m : 128 * m + 128].reshape(2, 64, 256)

            if e:
                for m, g in enumerate(gs):
                    pair = pl.ds(2 * g, 2)
                    send(f"sh{t}{i}{m}", PDS.at[t, pair], PDI.at[t, pair], sib)

    def share(t, i):
        gs = ((y,), ((y + 2) % 4,), ((y + 1) % 4, (y + 3) % 4))[i]
        index = names.setdefault(f"f{t}", len(names))
        for m, g in enumerate(gs):
            pair = pl.ds(2 * g, 2)
            arrive(f"sh{t}{i}{m}", PDI.at[t, pair], sib)
            for e in range(2):
                j = 2 * g + e
                add(PDO.at[t, j], PDO.at[t, j], PDI.at[t, j])

            @pl.when(g != z)
            def _():
                slot = (g - z + 4) % 4 - 1
                copy_of(index, PDO.at[t, pair], FR.at[t, slot], (xl * 4 + g, w)).start()

    def head_sum(t, e):
        total = PDO[t, 2 * z + e].astype(F32)
        for n in range(3):
            total = total + FR[t, n, e].astype(F32)
        return total

    def across(t):
        arrive(f"f{t}", FR.at[t], hdev(1))
        for n in range(1, 4):
            g = (z + n) % 4
            sent.append(
                copy_of(names[f"f{t}"], PDO.at[t, pl.ds(2 * g, 2)], FR.at[t, n - 1], (xl * 4 + g, w))
            )
        FS[t] = head_sum(t, 1 - xl).astype(BF)
        send(f"fx{t}", FS.at[t], FXR.at[t], hdev(4))

    def finish(t):
        total = head_sum(t, xl)
        arrive(f"fx{t}", FXR.at[t], hdev(4))
        total = total + FXR[t].astype(F32)
        rounded = total.astype(BF)
        out[1, 32 * t : 32 * t + 32, :] = rounded[0:32]
        out[1, 64 + 32 * t : 96 + 32 * t, :] = rounded[32:64]

    steps = {"in": (enter,)}
    for k in range(16):
        steps[f"u{k}"] = (untwist, k)
    for t in range(2):
        steps[f"at{t}"] = (attend, t)
        for dx, dy in OTHERS:
            steps[f"gf{t}{dx}{dy}"] = (gather_on, t, dx, dy)
        steps[f"op{t}"] = (project, t)
        steps[f"cm{t}"] = (combine, t)
        for k in range(1, 8):
            steps[f"xf{t}{k}"] = (spread, t, k)
        steps[f"xr{t}"] = (spread_end, t)
        steps[f"sq{t}"] = (squares, t)
        steps[f"sc{t}"] = (row_scale, t)
        for d in range(2):
            steps[f"ga{t}{d}"] = (a_piece, t, d)
            steps[f"gb{t}{d}"] = (b_piece, t, d)
            for s in range(3):
                steps[f"as{t}{d}{s + 1}"] = (a_step, t, d, s + 1)
                steps[f"bs{t}{d}{s}"] = (b_sum, t, d, s)
                steps[f"hb{t}{d}{s}"] = (hb_step, t, d, s)
            steps[f"bf{t}{d}"] = (b_end, t, d)
            steps[f"af{t}{d}"] = (a_end, t, d)
            for s in (0, 1):
                for q in "op":
                    steps[f"h{q}{t}{d}{s}"] = (ha_step, t, d, s, q)
            steps[f"hp{t}{d}9"] = (ha_step, t, d, 9, "p")
        for i in range(3):
            steps[f"dn{t}{i}"] = (down, t, i)
            steps[f"fz{t}{i}"] = (share, t, i)
        steps[f"fx{t}"] = (across, t)
        steps[f"fo{t}"] = (finish, t)
    assert sorted(steps) == sorted(ORDER)
    assert len(ORDER) == len(set(ORDER))
    for name in ORDER:
        step, *where = steps[name]
        step(*where)

    assert len(names) <= N_COPIES
    for cp in sent:
        cp.wait_send()


N_COPIES = 160


def layer(
    queries, fresh_keys, fresh_values, cached_keys, cached_values, context_len, tree_size, parents,
    residual, out_weight, gate_up_weight, down_weight,
):
    vm = pltpu.VMEM
    scratch = [
        vm((CTX, HD), BF),
        vm((CTX, HD), BF),
        vm((128, HD), BF),
        vm((128, HD), BF),
        vm((256, CTX + 128), F32),
        vm((256, CTX + 128), BF),
        vm((TREE, 128), F32),
        vm((2, 32, 1024), BF),
        vm((2, 16, 32, 1024), BF),
        vm((512, 2, HALF), BF),
        vm((512, 2, HALF), BF),
        vm((1024, 2 * HALF), BF),
        vm((2, HALF, 512), BF),
        vm((1024, 512), BF),
        vm((128, 512), BF),
        vm((2, 8, 64, 512), BF),
        vm((2, 7, 64, 512), BF),
        vm((2, 8, 64, 1024), BF),
        vm((2, 2, 4, 2, 64, A_W), BF),
        vm((2, 2, 4, 2, 64, B_W), BF),
        vm((2, 2, 3, 2, 64, A_W), BF),
        vm((2, 2, 64, A_W), BF),
        vm((2, 2, 4, 64, B_W), BF),
        vm((2, 2, 3, 64, B_W), BF),
        vm((2, 8, 8, 128), F32),
        vm((2, 7, 8, 128), F32),
        vm((2, 64, 128), F32),
        vm((2, 4, 2, 64, HALF), BF),
        vm((2, 8, 64, 512), BF),
        vm((2, 8, 64, 512), BF),
        vm((2, 8, 64, 512), BF),
        vm((2, 3, 2, 64, 512), BF),
        vm((2, 64, 512), BF),
        vm((2, 64, 512), BF),
        pltpu.SemaphoreType.DMA((6,)),
        pltpu.SemaphoreType.DMA((1,)),
        pltpu.SemaphoreType.DMA((N_COPIES,)),
    ]
    in_vmem = pl.BlockSpec(memory_space=pltpu.VMEM)
    in_smem = pl.BlockSpec(memory_space=pltpu.SMEM)
    in_hbm = pl.BlockSpec(memory_space=pl.ANY)
    both = pl.pallas_call(
        layer_kernel,
        out_shape=jax.ShapeDtypeStruct((2, 128, 512), BF),
        in_specs=[in_vmem] * 4 + [in_smem] * 2 + [in_hbm] * 6,
        out_specs=in_vmem,
        scratch_shapes=scratch,
        name="layer",
        compiler_params=pltpu.CompilerParams(
            collective_id=0, has_side_effects=True, vmem_limit_bytes=60 << 20
        ),
    )(
        queries, fresh_keys, fresh_values, parents, context_len, tree_size, cached_keys, cached_values,
        gate_up_weight, down_weight, out_weight, residual,
    )
    return both[0], both[1]


def solution(mesh):
    placed = (
        P("wide", "head"),
        P("wide", "head"),
        P("wide", "head"),
        P("wide", None, "head"),
        P("wide", None, "head"),
        P("wide"),
        P("wide"),
        P("wide", None),
        P(None, "wide"),
        P("head", "wide"),
        P("wide", None, "head"),
        P("head", "wide"),
    )
    return jax.shard_map(
        layer,
        mesh=mesh,
        in_specs=placed,
        out_specs=(P("head", "wide"), P("head", "wide")),
        check_vma=False,
    )
```

```python
import math

import jax
import jax.numpy as jnp
from jax import lax
from jax.experimental import pallas as pl
from jax.experimental.pallas import tpu as pltpu
from jax.sharding import PartitionSpec as P

D = 8192
HD = 128
CTX = 2048
TREE = 64

epsilon = 1e-05

BF = jnp.bfloat16
F32 = jnp.float32
MESH = pl.DeviceIdType.MESH

A_U = 512
B_U = 384
A_W = 2 * A_U
B_W = 2 * B_U
HALF = 2 * A_U + 2 * B_U
H_OFF = (0, A_U, 2 * A_U, 2 * A_U + B_U)
OTHERS = ((0, 1), (0, 3), (1, 0), (0, 2), (1, 1), (1, 3), (1, 2))

NR = (16, 32, 16)
ROW0 = (0, 16, 48)
TWO_HOPS = ()

ORDER = (
    0, 17, 81, 1, 145, 21, 19, 18, 24, 2, 23, 22, 20, 3, 84, 4, 85, 83, 87, 86, 82, 25, 88, 5, 6,
    89, 149, 148, 7, 146, 151, 8, 152, 9, 26, 10, 11, 150, 12, 90, 13, 147, 30, 14, 29, 33, 32, 31,
    27, 28, 15, 153, 34, 91, 16, 93, 56, 95, 92, 55, 96, 97, 94, 37, 154, 98, 101, 57, 120, 39, 58,
    155, 119, 161, 160, 157, 156, 158, 38, 159, 102, 122, 61, 162, 103, 42, 35, 121, 99, 166, 106,
    183, 165, 124, 40, 104, 100, 125, 168, 60, 109, 185, 167, 64, 127, 43, 107, 45, 128, 63, 113,
    171, 36, 163, 184, 188, 49, 110, 46, 131, 130, 186, 118, 112, 191, 67, 170, 66, 164, 48, 123,
    132, 136, 105, 189, 114, 115, 174, 137, 54, 173, 126, 108, 133, 192, 195, 72, 134, 73, 117, 177,
    116, 138, 176, 194, 129, 111, 41, 59, 74, 135, 139, 68, 182, 51, 187, 200, 69, 196, 50, 62, 201,
    44, 140, 169, 178, 179, 141, 197, 190, 71, 172, 52, 70, 53, 47, 198, 180, 75, 65, 181, 142, 199,
    175, 193, 203, 76, 202, 77, 204, 205, 78, 143, 206, 79, 207, 144, 80, 208,
)


def layer_kernel(
    queries, fresh_k, fresh_v, parents, length, live, keys_hbm, values_hbm,
    gw, dw, wo_hbm, res_hbm,
    out,
    KS, VS, FK, FV, S, PR, TB, ATT,
    G, R0, R1, WC, DD, WO, RES, PP, RB, X, PA, PB, RA, RAX, RBX, RBY, SQ, SQR, SC, H, PDO, PDS, PDI, FR, FS, FXR, OS, OXR,
    lsem, ssem, rsem,
):
    h = lax.axis_index("head")
    w = lax.axis_index("wide")
    xh = w // 8
    y = (w // 2) % 4
    c = w % 2
    flip = 1 - 2 * c
    xo = 1 - xh

    def wide(dxh, dy):
        return (((xh + dxh + 2) % 2) * 4 + (y + dy + 4) % 4) * 2 + c

    sib = (h, w + flip)
    xl = h // 4
    z = h % 4

    def place(j):
        return 2 * (j % 4) + j // 4

    def wdev(dxh, dy):
        return (h, wide(dxh, dy))

    def hdev(k):
        return ((h + k) % 8, w)

    def zdev(n):
        return (xl * 4 + (z + n) % 4, w)

    names = {}
    sent = []

    def copy_of(i, src, dst, dev):
        return pltpu.make_async_remote_copy(
            src_ref=src, dst_ref=dst, send_sem=ssem.at[0], recv_sem=rsem.at[i],
            device_id=dev, device_id_type=MESH,
        )

    def send(name, src, dst, dev):
        i = names.setdefault(name, len(names))
        cp = copy_of(i, src, dst, dev)
        cp.start()
        sent.append(cp)

    def arrive(name, dst, dev):
        copy_of(names[name], dst, dst, dev).wait_recv()

    mine = pl.ds(pl.multiple_of(c * HALF, 128), HALF)
    other = pl.ds(pl.multiple_of((1 - c) * HALF, 128), HALF)
    loads = [
        pltpu.make_async_copy(keys_hbm.at[0], KS, lsem.at[0]),
        pltpu.make_async_copy(values_hbm.at[0], VS, lsem.at[1]),
        pltpu.make_async_copy(gw.at[:, :, mine], R0, lsem.at[2]),
        pltpu.make_async_copy(wo_hbm, WO, lsem.at[3]),
        pltpu.make_async_copy(
            res_hbm.at[pl.ds(pl.multiple_of(h * 128, 128), 128), :], RES, lsem.at[4]
        ),
        pltpu.make_async_copy(dw.at[mine, :], DD.at[0], lsem.at[5]),
    ]
    for cp in loads:
        cp.start()

    partners = [sib]
    partners += [wdev(dx, dy) for dx, dy in OTHERS]
    partners += [hdev(k) for k in range(1, 8)]
    barrier = pltpu.get_barrier_semaphore()
    for dev in partners:
        pl.semaphore_signal(barrier, inc=1, device_id=dev, device_id_type=MESH)

    def enter():
        pl.semaphore_wait(barrier, len(partners))
        send("s_gw", gw.at[:, :, other], R1, sib)

    node = lax.broadcasted_iota(jnp.int32, (TREE, TREE), 0)
    child = lax.broadcasted_iota(jnp.int32, (TREE, TREE), 1)
    linked = (parents[...] == node) | (node == child)
    reached = jnp.where(linked, 1.0, 0.0).astype(BF)
    for squaring in range(6):
        reached = jnp.minimum(jnp.dot(reached, reached, preferred_element_type=F32), 1.0).astype(BF)
    same = jnp.where(node == child, 1.0, 0.0).astype(BF)
    visible = lax.dot_general(reached, same, (((0,), (0,)), ((), ())), preferred_element_type=F32)
    TB[...] = jnp.full((TREE, 128), -1e30, F32)
    TB[:, 0:TREE] = jnp.where((visible > 0.5) & (child < live[0]), 0.0, -1e30)
    FK[0:TREE] = fresh_k[...]
    FK[TREE:128] = jnp.zeros((128 - TREE, HD), BF)
    FV[0:TREE] = fresh_v[...]
    FV[TREE:128] = jnp.zeros((128 - TREE, HD), BF)
    positions = lax.broadcasted_iota(jnp.int32, (1, CTX), 1)
    cache_bias = jnp.where(positions < length[0], 0.0, -1e30)
    score_scale = math.log2(math.e) / math.sqrt(HD)

    def attend(t):
        if t == 0:
            loads[0].wait()
        r0, nr = ROW0[t], NR[t]
        m8 = 8 * nr
        q = jnp.concatenate([queries[r0 : r0 + nr, j * HD : (j + 1) * HD] for j in range(8)], axis=0)
        trans = (((1,), (1,)), ((), ()))

        @pl.loop(0, CTX // 512)
        def _(i):
            n = pl.ds(pl.multiple_of(i * 512, 512), 512)
            S[0:m8, n] = lax.dot_general(q, KS[n, :], trans, preferred_element_type=F32)

        S[0:m8, CTX : CTX + 128] = lax.dot_general(q, FK[...], trans, preferred_element_type=F32)
        if t == 0:
            loads[1].wait()
        alive = lax.broadcasted_iota(jnp.int32, (nr, 1), 0) + r0 < live[0]
        denominators = []
        strips = nr // 16
        for j in range(8 * strips):
            r = slice(16 * j, 16 * j + 16)
            n0 = r0 + 16 * (j % strips)
            cache = S[r, 0:CTX] + cache_bias
            tree = S[r, CTX : CTX + 128] + TB[n0 : n0 + 16, :]
            row_max = jnp.maximum(
                jnp.max(cache, axis=1, keepdims=True), jnp.max(tree, axis=1, keepdims=True)
            )
            cache = jnp.exp2((cache - row_max) * score_scale)
            tree = jnp.exp2((tree - row_max) * score_scale)
            denominators.append(
                jnp.sum(cache, axis=1, keepdims=True) + jnp.sum(tree, axis=1, keepdims=True)
            )
            PR[r, 0:CTX] = cache.astype(BF)
            PR[r, CTX : CTX + 128] = tree.astype(BF)
        mixed = jnp.dot(PR[0:m8, 0:CTX], VS[...], preferred_element_type=F32)
        mixed = mixed + jnp.dot(PR[0:m8, CTX : CTX + 128], FV[...], preferred_element_type=F32)
        for j in range(8):
            below = jnp.concatenate(denominators[strips * j : strips * j + strips], axis=0)
            part = mixed[nr * j : nr * j + nr] / below
            ATT[t][:, j * HD : (j + 1) * HD] = jnp.where(alive, part, 0.0).astype(BF)
        for dx, dy in OTHERS:
            send(f"g{t}{dx}{dy}", ATT[t], G[t].at[w], wdev(dx, dy))
        send(f"gc{t}", ATT[t], G[t].at[w], sib)
        G[t][w] = ATT[t][...]

    def gather_on(t, dx, dy):
        src = wide(-dx, -dy)
        arrive(f"g{t}{dx}{dy}", G[t].at[src], wdev(-dx, -dy))
        send(f"gc{t}", G[t].at[src], G[t].at[src], sib)

    def untwist(k):
        if k == 0:
            loads[2].wait()
        if k == 8:
            arrive("s_gw", R1, sib)
        raw = R0 if k < 8 else R1
        i = k % 8
        b = raw[64 * i : 64 * i + 64]
        gate, up = b[:, 0, :], b[:, 1, :]
        o = slice(64 * k, 64 * k + 64)
        for p in range(4):
            n = A_U if p < 2 else B_U
            u = H_OFF[p]
            WC[o, 2 * u : 2 * u + n] = gate[:, u : u + n]
            WC[o, 2 * u + n : 2 * u + 2 * n] = up[:, u : u + n]

    def project(t):
        arrive(f"gc{t}", G[t].at[0:8], sib)
        if t == 0:
            loads[3].wait()
        L = 2 * NR[t]
        rows = G[t][...].reshape(8 * L, 1024)
        part = jnp.dot(rows, WO[...], preferred_element_type=F32).astype(BF).reshape(8, L, 512)
        for j in range(8):
            PP[t][place(j)] = part[j]
        if t == len(NR) - 1:
            send("s_dw", dw.at[other, :], DD.at[1], sib)
        if t in TWO_HOPS:
            for n in (1, 3, 2):
                pair = pl.ds(2 * ((z + n) % 4), 2)
                send(f"o{t}", PP[t].at[pair], RB[t].at[2 * n - 2 : 2 * n], zdev(n))
            return
        for k in range(1, 8):
            send(f"o{t}", PP[t].at[place((h + k) % 8)], RB[t].at[k - 1], hdev(k))

    def z_sum(t, e):
        total = PP[t][2 * z + e].astype(F32)
        for n in range(3):
            total = total + RB[t][2 * n + e].astype(F32)
        return total

    def other_half(t):
        arrive(f"o{t}", RB[t].at[0:6], hdev(1))
        OS[t][...] = z_sum(t, 1 - xl).astype(BF)
        send(f"ox{t}", OS[t], OXR[t], hdev(4))

    def combine(t):
        if t == 0:
            loads[4].wait()
        r0, nr = ROW0[t], NR[t]
        rows = (slice(r0, r0 + nr), slice(64 + r0, 64 + r0 + nr))
        total = jnp.concatenate([RES[r, :] for r in rows], axis=0).astype(F32)
        if t in TWO_HOPS:
            total = total + z_sum(t, xl)
            arrive(f"ox{t}", OXR[t], hdev(4))
            total = total + OXR[t][...].astype(F32)
        else:
            total = total + PP[t][place(h)].astype(F32)
            arrive(f"o{t}", RB[t], hdev(1))
            for k in range(7):
                total = total + RB[t][k].astype(F32)
        rounded = total.astype(BF)
        own = X[t].at[place(h), :, 0:512]
        own[...] = rounded
        if t in TWO_HOPS:
            send(f"xx_{t}", own, own, hdev(4))
        else:
            for k in range(1, 8):
                send(f"x{t}{k}", own, own, hdev(k))
        send(f"xc{t}", own, X[t].at[place(h), :, 512:1024], sib)
        out[0, rows[0], :] = rounded[0:nr]
        out[0, rows[1], :] = rounded[nr : 2 * nr]

    def spread_pair(t):
        one = 2 * z + 1 - xl
        arrive(f"xx_{t}", X[t].at[one, :, 0:512], hdev(4))
        both = X[t].at[pl.ds(2 * z, 2), :, 0:512]
        for n in (1, 3, 2):
            send(f"x{t}{n}", both, both, zdev(n))
        send(f"xc{t}", X[t].at[one, :, 0:512], X[t].at[one, :, 512:1024], sib)

    def spread(t, k):
        if t in TWO_HOPS:
            j = pl.ds(2 * ((z + 4 - k) % 4), 2)
            arrive(f"x{t}{k}", X[t].at[j, :, 0:512], zdev(4 - k))
        else:
            j = place((h + 8 - k) % 8)
            arrive(f"x{t}{k}", X[t].at[j, :, 0:512], hdev(8 - k))
        send(f"xc{t}", X[t].at[j, :, 0:512], X[t].at[j, :, 512:1024], sib)

    def spread_end(t):
        arrive(f"xc{t}", X[t].at[:, :, 512:1024], sib)

    step_dev = [wdev(0, 1), wdev(0, 3)]
    from_dev = [wdev(0, 3), wdev(0, 1)]
    xdev = wdev(1, 0)

    def first(d, s):
        return (y + 3 - s + 4) % 4 if d == 0 else (y + 1 + s) % 4

    def product(t, out, col0, width):
        @pl.loop(0, width // 256)
        def _(i):
            rows = X[t][...].reshape(16 * NR[t], 1024)
            cols = pl.ds(pl.multiple_of(col0 + i * 256, 256), 256)
            part = jnp.dot(rows, WC[:, cols], preferred_element_type=F32).astype(BF)
            out[:, :, :, pl.ds(pl.multiple_of(i * 256, 256), 256)] = part.reshape(4, 2, 2 * NR[t], 256)

    def a_piece(t, d):
        product(t, PA[t].at[d], d * A_W, A_W)
        send(f"a{t}{d}0", PA[t].at[d, first(d, 0)], RA[t].at[d, 0], step_dev[d])

    def b_piece(t, d):
        product(t, PB[t].at[d], 2 * A_W + d * B_W, B_W)
        for s in range(4):
            g = first(d, s)
            send(f"bx{t}{d}{s}", PB[t].at[d, g, xo], RBX[t].at[d, s], xdev)

    def squares(t):
        ones = jnp.ones((8, 1024), BF)
        for b in range(8):
            v = X[t][b].astype(F32)
            part = lax.dot_general(
                ones, (v * v).astype(BF), (((1,), (1,)), ((), ())), preferred_element_type=F32
            )
            SQ[t][b] = jnp.concatenate([part] * (64 // NR[t]), axis=1)
        for n, (dx, dy) in enumerate(OTHERS):
            b = ((y + dy) % 4) * 2 + (xh + dx) % 2
            send(f"q{t}", SQ[t].at[b], SQR[t].at[n], wdev(dx, dy))

    def row_scale(t):
        total = SQ[t][y * 2 + xh]
        arrive(f"q{t}", SQR[t], wdev(0, 1))
        for n in range(7):
            total = total + SQR[t][n]
        scale = lax.rsqrt(jnp.transpose(total)[0 : 2 * NR[t], 0:1] / D + epsilon)
        SC[t][...] = jnp.broadcast_to(scale, (2 * NR[t], 128))

    def add(out, left, right):
        for i in range(out.shape[0] // 32):
            r = slice(32 * i, 32 * i + 32)
            out[r, :] = (left[r, :].astype(F32) + right[r, :].astype(F32)).astype(BF)

    def a_step(t, d, s):
        g = first(d, s)
        arrive(f"a{t}{d}{s - 1}", RA[t].at[d, s - 1], from_dev[d])
        for e in range(2):
            add(PA[t].at[d, g, e], PA[t].at[d, g, e], RA[t].at[d, s - 1, e])
        if s < 3:
            send(f"a{t}{d}{s}", PA[t].at[d, g], RA[t].at[d, s], step_dev[d])
        else:
            send(f"xx{t}{d}", PA[t].at[d, y, xo], RAX[t].at[d], xdev)

    def b_sum(t, d, s):
        g = first(d, s)
        out = PB[t].at[d, g, xh]
        arrive(f"bx{t}{d}{s}", RBX[t].at[d, s], xdev)
        add(out, out, RBX[t].at[d, s])
        if s and s < 3:
            arrive(f"b{t}{d}{s - 1}", RBY[t].at[d, s - 1], from_dev[d])
            add(out, out, RBY[t].at[d, s - 1])
        if s < 3:
            send(f"b{t}{d}{s}", out, RBY[t].at[d, s], step_dev[d])

    def gated(t, left, right, n, col0):
        scale = SC[t][:, 0:1]
        gate = (left[:, 0:n].astype(F32) + right[:, 0:n].astype(F32)) * scale
        up = (left[:, n : 2 * n].astype(F32) + right[:, n : 2 * n].astype(F32)) * scale
        H[t][y, xh, :, col0 : col0 + n] = (gate / (1.0 + jnp.exp(-gate)) * up).astype(BF)

    def cols(part, d):
        o = H_OFF[2 * part + d]
        return slice(o, o + (A_U, B_U)[part])

    def b_end(t, d):
        b_sum(t, d, 3)
        arrive(f"b{t}{d}2", RBY[t].at[d, 2], from_dev[d])
        gated(t, PB[t].at[d, y, xh], RBY[t].at[d, 2], B_U, H_OFF[2 + d])
        piece = H[t].at[y, xh, :, cols(1, d)]
        send(f"hb{t}{d}0", piece, piece, step_dev[d])
        send(f"hx{t}{d}9", piece, piece, xdev)

    def hb_step(t, d, s):
        piece = H[t].at[first(d, s), xh, :, cols(1, d)]
        arrive(f"hb{t}{d}{s}", piece, from_dev[d])
        if s < 2:
            send(f"hb{t}{d}{s + 1}", piece, piece, step_dev[d])
        send(f"hx{t}{d}{s}", piece, piece, xdev)

    def a_end(t, d):
        arrive(f"xx{t}{d}", RAX[t].at[d], xdev)
        gated(t, PA[t].at[d, y, xh], RAX[t].at[d], A_U, H_OFF[d])
        piece = H[t].at[y, xh, :, cols(0, d)]
        send(f"ho{t}{d}0", piece, piece, step_dev[d])
        send(f"hp{t}{d}9", piece, piece, xdev)

    def ha_step(t, d, s, q):
        if s == 9:
            piece = H[t].at[y, xo, :, cols(0, d)]
            arrive(f"hp{t}{d}9", piece, xdev)
            send(f"hp{t}{d}0", piece, piece, step_dev[d])
            return
        piece = H[t].at[first(d, s), xh if q == "o" else xo, :, cols(0, d)]
        arrive(f"h{q}{t}{d}{s}", piece, from_dev[d])
        if s < 2:
            send(f"h{q}{t}{d}{s + 1}", piece, piece, step_dev[d])

    down_ready = []

    def down(t, i):
        if not down_ready:
            loads[5].wait()
            arrive("s_dw", DD.at[1], sib)
            down_ready.append(True)
        steps = ((9,), (1,), (0, 2))[i]
        for s in steps:
            for d in range(2):
                g = y if s == 9 else first(d, s)
                arrive(f"hx{t}{d}{s}", H[t].at[g, xo, :, cols(1, d)], xdev)
                if s == 2:
                    ha_step(t, d, 2, "o")
                    ha_step(t, d, 2, "p")
        gs = ((y,), ((y + 2) % 4,), ((y + 1) % 4, (y + 3) % 4))[i]
        for e, out in ((1, PDS), (0, PDO)):
            @pl.loop(0, 2)
            def _(n):
                n = pl.ds(pl.multiple_of(n * 256, 256), 256)
                rows = jnp.concatenate([H[t][g].reshape(4 * NR[t], HALF) for g in gs], axis=0)
                part = jnp.dot(rows, DD[e, :, n], preferred_element_type=F32).astype(BF)
                for m, g in enumerate(gs):
                    block = part[4 * NR[t] * m : 4 * NR[t] * (m + 1)].reshape(2, 2 * NR[t], 256)
                    out[t][pl.ds(2 * g, 2), :, n] = block

            if e:
                for m, g in enumerate(gs):
                    pair = pl.ds(2 * g, 2)
                    send(f"sh{t}{i}{m}", PDS[t].at[pair], PDI[t].at[pair], sib)

    def share(t, i):
        gs = ((y,), ((y + 2) % 4,), ((y + 1) % 4, (y + 3) % 4))[i]
        index = names.setdefault(f"f{t}", len(names))
        for m, g in enumerate(gs):
            pair = pl.ds(2 * g, 2)
            arrive(f"sh{t}{i}{m}", PDI[t].at[pair], sib)
            for e in range(2):
                j = 2 * g + e
                add(PDO[t].at[j], PDO[t].at[j], PDI[t].at[j])

            @pl.when(g != z)
            def _():
                slot = (g - z + 4) % 4 - 1
                copy_of(index, PDO[t].at[pair], FR[t].at[slot], (xl * 4 + g, w)).start()

    def head_sum(t, e):
        total = PDO[t][2 * z + e].astype(F32)
        for n in range(3):
            total = total + FR[t][n, e].astype(F32)
        return total

    def across(t):
        arrive(f"f{t}", FR[t], hdev(1))
        for n in range(1, 4):
            g = (z + n) % 4
            sent.append(
                copy_of(names[f"f{t}"], PDO[t].at[pl.ds(2 * g, 2)], FR[t].at[n - 1], (xl * 4 + g, w))
            )
        FS[t][...] = head_sum(t, 1 - xl).astype(BF)
        send(f"fx{t}", FS[t], FXR[t], hdev(4))

    def finish(t):
        total = head_sum(t, xl)
        arrive(f"fx{t}", FXR[t], hdev(4))
        total = total + FXR[t][...].astype(F32)
        rounded = total.astype(BF)
        r0, nr = ROW0[t], NR[t]
        out[1, r0 : r0 + nr, :] = rounded[0:nr]
        out[1, 64 + r0 : 64 + r0 + nr, :] = rounded[nr : 2 * nr]

    steps = {"in": (enter,)}
    for k in range(16):
        steps[f"u{k}"] = (untwist, k)
    for t in range(len(NR)):
        steps[f"at{t}"] = (attend, t)
        for dx, dy in OTHERS:
            steps[f"gf{t}{dx}{dy}"] = (gather_on, t, dx, dy)
        steps[f"op{t}"] = (project, t)
        steps[f"cm{t}"] = (combine, t)
        if t in TWO_HOPS:
            steps[f"or{t}"] = (other_half, t)
            steps[f"xp{t}"] = (spread_pair, t)
        for k in range(1, 4 if t in TWO_HOPS else 8):
            steps[f"xf{t}{k}"] = (spread, t, k)
        steps[f"xr{t}"] = (spread_end, t)
        steps[f"sq{t}"] = (squares, t)
        steps[f"sc{t}"] = (row_scale, t)
        for d in range(2):
            steps[f"ga{t}{d}"] = (a_piece, t, d)
            steps[f"gb{t}{d}"] = (b_piece, t, d)
            for s in range(3):
                steps[f"as{t}{d}{s + 1}"] = (a_step, t, d, s + 1)
                steps[f"bs{t}{d}{s}"] = (b_sum, t, d, s)
                steps[f"hb{t}{d}{s}"] = (hb_step, t, d, s)
            steps[f"bf{t}{d}"] = (b_end, t, d)
            steps[f"af{t}{d}"] = (a_end, t, d)
            for s in (0, 1):
                for q in "op":
                    steps[f"h{q}{t}{d}{s}"] = (ha_step, t, d, s, q)
            steps[f"hp{t}{d}9"] = (ha_step, t, d, 9, "p")
        for i in range(3):
            steps[f"dn{t}{i}"] = (down, t, i)
            steps[f"fz{t}{i}"] = (share, t, i)
        steps[f"fx{t}"] = (across, t)
        steps[f"fo{t}"] = (finish, t)
    table = list(steps.values())
    assert sorted(ORDER) == list(range(len(table)))
    for number in ORDER:
        step, *where = table[number]
        step(*where)

    assert len(names) <= N_COPIES
    for cp in sent:
        cp.wait_send()


N_COPIES = 224


def layer(
    queries, fresh_keys, fresh_values, cached_keys, cached_values, context_len, tree_size, parents,
    residual, out_weight, gate_up_weight, down_weight,
):
    vm = pltpu.VMEM

    def parts(per_row, *shape):
        return tuple(vm(tuple(x or per_row * n for x in shape), BF) for n in NR)

    scratch = [
        vm((CTX, HD), BF),
        vm((CTX, HD), BF),
        vm((128, HD), BF),
        vm((128, HD), BF),
        vm((256, CTX + 128), F32),
        vm((256, CTX + 128), BF),
        vm((TREE, 128), F32),
        parts(1, 0, 1024),
        parts(1, 16, 0, 1024),
        vm((512, 2, HALF), BF),
        vm((512, 2, HALF), BF),
        vm((1024, 2 * HALF), BF),
        vm((2, HALF, 512), BF),
        vm((1024, 512), BF),
        vm((128, 512), BF),
        parts(2, 8, 0, 512),
        parts(2, 7, 0, 512),
        parts(2, 8, 0, 1024),
        parts(2, 2, 4, 2, 0, A_W),
        parts(2, 2, 4, 2, 0, B_W),
        parts(2, 2, 3, 2, 0, A_W),
        parts(2, 2, 0, A_W),
        parts(2, 2, 4, 0, B_W),
        parts(2, 2, 3, 0, B_W),
        tuple(vm((8, 8, 128), F32) for n in NR),
        tuple(vm((7, 8, 128), F32) for n in NR),
        tuple(vm((2 * n, 128), F32) for n in NR),
        parts(2, 4, 2, 0, HALF),
        parts(2, 8, 0, 512),
        parts(2, 8, 0, 512),
        parts(2, 8, 0, 512),
        parts(2, 3, 2, 0, 512),
        parts(2, 0, 512),
        parts(2, 0, 512),
        parts(2, 0, 512),
        parts(2, 0, 512),
        pltpu.SemaphoreType.DMA((6,)),
        pltpu.SemaphoreType.DMA((1,)),
        pltpu.SemaphoreType.DMA((N_COPIES,)),
    ]
    in_vmem = pl.BlockSpec(memory_space=pltpu.VMEM)
    in_smem = pl.BlockSpec(memory_space=pltpu.SMEM)
    in_hbm = pl.BlockSpec(memory_space=pl.ANY)
    both = pl.pallas_call(
        layer_kernel,
        out_shape=jax.ShapeDtypeStruct((2, 128, 512), BF),
        in_specs=[in_vmem] * 4 + [in_smem] * 2 + [in_hbm] * 6,
        out_specs=in_vmem,
        scratch_shapes=scratch,
        name="layer",
        compiler_params=pltpu.CompilerParams(
            collective_id=0, has_side_effects=True, vmem_limit_bytes=60 << 20
        ),
    )(
        queries, fresh_keys, fresh_values, parents, context_len, tree_size, cached_keys, cached_values,
        gate_up_weight, down_weight, out_weight, residual,
    )
    return both[0], both[1]


def solution(mesh):
    placed = (
        P("wide", "head"),
        P("wide", "head"),
        P("wide", "head"),
        P("wide", None, "head"),
        P("wide", None, "head"),
        P("wide"),
        P("wide"),
        P("wide", None),
        P(None, "wide"),
        P("head", "wide"),
        P("wide", None, "head"),
        P("head", "wide"),
    )
    return jax.shard_map(
        layer,
        mesh=mesh,
        in_specs=placed,
        out_specs=(P("head", "wide"), P("head", "wide")),
        check_vma=False,
    )
```

```python
import math

import jax
import jax.numpy as jnp
from jax import lax
from jax.experimental import pallas as pl
from jax.experimental.pallas import tpu as pltpu
from jax.sharding import PartitionSpec as P

D = 8192
HD = 128
CTX = 2048
TREE = 64

epsilon = 1e-05

BF = jnp.bfloat16
F32 = jnp.float32
MESH = pl.DeviceIdType.MESH

A_U = 512
B_U = 384
A_W = 2 * A_U
B_W = 2 * B_U
HALF = 2 * A_U + 2 * B_U
H_OFF = (0, A_U, 2 * A_U, 2 * A_U + B_U)
OTHERS = ((0, 1), (0, 3), (1, 0), (0, 2), (1, 1), (1, 3), (1, 2))

NR = (16, 32, 16)
ROW0 = (0, 16, 48)
LAST = len(NR) - 1
TWO_HOPS = ()

ORDER = (
    0, 17, 81, 145, 22, 20, 1, 2, 19, 23, 21, 82, 18, 24, 3, 4, 25, 85, 83, 86, 88, 84, 87, 5, 6,
    150, 89, 152, 147, 151, 7, 148, 146, 149, 8, 26, 153, 9, 10, 11, 90, 12, 27, 13, 32, 28, 30, 29,
    31, 14, 33, 15, 16, 34, 37, 56, 92, 55, 95, 91, 93, 94, 96, 97, 38, 39, 58, 98, 101, 57, 154,
    61, 119, 42, 120, 64, 40, 157, 99, 158, 103, 122, 161, 155, 160, 121, 156, 159, 102, 162, 165,
    184, 183, 106, 166, 167, 60, 124, 100, 35, 43, 104, 163, 186, 170, 109, 168, 125, 185, 127, 107,
    46, 128, 63, 113, 188, 189, 36, 173, 45, 110, 130, 67, 114, 131, 164, 171, 191, 112, 177, 192,
    123, 118, 48, 132, 49, 105, 66, 136, 174, 195, 194, 115, 126, 137, 108, 133, 41, 182, 176, 116,
    50, 134, 54, 111, 129, 59, 72, 187, 44, 68, 200, 73, 135, 169, 62, 117, 139, 138, 69, 52, 178,
    196, 190, 47, 51, 197, 172, 70, 179, 140, 141, 53, 71, 198, 180, 65, 193, 75, 199, 181, 175,
    142, 77, 201, 76, 78, 74, 143, 202, 79, 144, 203, 80,
)


def layer_kernel(
    queries, fresh_k, fresh_v, parents, length, live, keys_hbm, values_hbm,
    gw, dw, wo_hbm, res_hbm,
    out,
    KS, VS, FK, FV, S, PR, TB, ATT,
    G, R0, R1, WC, DD, WO, RES, PP, RB, X, PA, PB, RA, RAX, RBX, RBY, SQ, SQR, SC, H, PDO, PDS, PDI, FR, FS, FXR, OS, OXR,
    lsem, ssem, rsem,
):
    h = lax.axis_index("head")
    w = lax.axis_index("wide")
    xh = w // 8
    y = (w // 2) % 4
    c = w % 2
    flip = 1 - 2 * c
    xo = 1 - xh

    def wide(dxh, dy):
        return (((xh + dxh + 2) % 2) * 4 + (y + dy + 4) % 4) * 2 + c

    sib = (h, w + flip)
    xl = h // 4
    z = h % 4

    def place(j):
        return 2 * (j % 4) + j // 4

    def wdev(dxh, dy):
        return (h, wide(dxh, dy))

    def hdev(k):
        return ((h + k) % 8, w)

    def zdev(n):
        return (xl * 4 + (z + n) % 4, w)

    names = {}
    sent = []

    def copy_of(i, src, dst, dev):
        return pltpu.make_async_remote_copy(
            src_ref=src, dst_ref=dst, send_sem=ssem.at[0], recv_sem=rsem.at[i],
            device_id=dev, device_id_type=MESH,
        )

    def send(name, src, dst, dev):
        i = names.setdefault(name, len(names))
        cp = copy_of(i, src, dst, dev)
        cp.start()
        sent.append(cp)

    def arrive(name, dst, dev):
        copy_of(names[name], dst, dst, dev).wait_recv()

    mine = pl.ds(pl.multiple_of(c * HALF, 128), HALF)
    other = pl.ds(pl.multiple_of((1 - c) * HALF, 128), HALF)
    loads = [
        pltpu.make_async_copy(keys_hbm.at[0], KS, lsem.at[0]),
        pltpu.make_async_copy(values_hbm.at[0], VS, lsem.at[1]),
        pltpu.make_async_copy(gw.at[:, :, mine], R0, lsem.at[2]),
        pltpu.make_async_copy(wo_hbm, WO, lsem.at[3]),
        pltpu.make_async_copy(
            res_hbm.at[pl.ds(pl.multiple_of(h * 128, 128), 128), :], RES, lsem.at[4]
        ),
        pltpu.make_async_copy(dw.at[mine, :], DD.at[0], lsem.at[5]),
    ]
    for cp in loads:
        cp.start()

    partners = [sib]
    partners += [wdev(dx, dy) for dx, dy in OTHERS]
    partners += [hdev(k) for k in range(1, 8)]
    barrier = pltpu.get_barrier_semaphore()
    for dev in partners:
        pl.semaphore_signal(barrier, inc=1, device_id=dev, device_id_type=MESH)

    def enter():
        pl.semaphore_wait(barrier, len(partners))
        send("s_gw", gw.at[:, :, other], R1, sib)

    node = lax.broadcasted_iota(jnp.int32, (TREE, TREE), 0)
    child = lax.broadcasted_iota(jnp.int32, (TREE, TREE), 1)
    linked = (parents[...] == node) | (node == child)
    reached = jnp.where(linked, 1.0, 0.0).astype(BF)
    for squaring in range(6):
        reached = jnp.minimum(jnp.dot(reached, reached, preferred_element_type=F32), 1.0).astype(BF)
    same = jnp.where(node == child, 1.0, 0.0).astype(BF)
    visible = lax.dot_general(reached, same, (((0,), (0,)), ((), ())), preferred_element_type=F32)
    TB[...] = jnp.full((TREE, 128), -1e30, F32)
    TB[:, 0:TREE] = jnp.where((visible > 0.5) & (child < live[0]), 0.0, -1e30)
    FK[0:TREE] = fresh_k[...]
    FK[TREE:128] = jnp.zeros((128 - TREE, HD), BF)
    FV[0:TREE] = fresh_v[...]
    FV[TREE:128] = jnp.zeros((128 - TREE, HD), BF)
    positions = lax.broadcasted_iota(jnp.int32, (1, CTX), 1)
    cache_bias = jnp.where(positions < length[0], 0.0, -1e30)
    score_scale = math.log2(math.e) / math.sqrt(HD)

    def attend(t):
        if t == 0:
            loads[0].wait()
        r0, nr = ROW0[t], NR[t]
        m8 = 8 * nr
        q = jnp.concatenate([queries[r0 : r0 + nr, j * HD : (j + 1) * HD] for j in range(8)], axis=0)
        trans = (((1,), (1,)), ((), ()))

        @pl.loop(0, CTX // 512)
        def _(i):
            n = pl.ds(pl.multiple_of(i * 512, 512), 512)
            S[0:m8, n] = lax.dot_general(q, KS[n, :], trans, preferred_element_type=F32)

        S[0:m8, CTX : CTX + 128] = lax.dot_general(q, FK[...], trans, preferred_element_type=F32)
        if t == 0:
            loads[1].wait()
        alive = lax.broadcasted_iota(jnp.int32, (nr, 1), 0) + r0 < live[0]
        denominators = []
        strips = nr // 16
        for j in range(8 * strips):
            r = slice(16 * j, 16 * j + 16)
            n0 = r0 + 16 * (j % strips)
            cache = S[r, 0:CTX] + cache_bias
            tree = S[r, CTX : CTX + 128] + TB[n0 : n0 + 16, :]
            row_max = jnp.maximum(
                jnp.max(cache, axis=1, keepdims=True), jnp.max(tree, axis=1, keepdims=True)
            )
            cache = jnp.exp2((cache - row_max) * score_scale)
            tree = jnp.exp2((tree - row_max) * score_scale)
            denominators.append(
                jnp.sum(cache, axis=1, keepdims=True) + jnp.sum(tree, axis=1, keepdims=True)
            )
            PR[r, 0:CTX] = cache.astype(BF)
            PR[r, CTX : CTX + 128] = tree.astype(BF)
        mixed = jnp.dot(PR[0:m8, 0:CTX], VS[...], preferred_element_type=F32)
        mixed = mixed + jnp.dot(PR[0:m8, CTX : CTX + 128], FV[...], preferred_element_type=F32)
        for j in range(8):
            below = jnp.concatenate(denominators[strips * j : strips * j + strips], axis=0)
            part = mixed[nr * j : nr * j + nr] / below
            ATT[t][:, j * HD : (j + 1) * HD] = jnp.where(alive, part, 0.0).astype(BF)
        for dx, dy in OTHERS:
            send(f"g{t}{dx}{dy}", ATT[t], G[t].at[w], wdev(dx, dy))
        send(f"gc{t}", ATT[t], G[t].at[w], sib)
        G[t][w] = ATT[t][...]

    def gather_on(t, dx, dy):
        src = wide(-dx, -dy)
        arrive(f"g{t}{dx}{dy}", G[t].at[src], wdev(-dx, -dy))
        send(f"gc{t}", G[t].at[src], G[t].at[src], sib)

    def untwist(k):
        if k == 0:
            loads[2].wait()
        if k == 8:
            arrive("s_gw", R1, sib)
        raw = R0 if k < 8 else R1
        i = k % 8
        b = raw[64 * i : 64 * i + 64]
        gate, up = b[:, 0, :], b[:, 1, :]
        o = slice(64 * k, 64 * k + 64)
        for p in range(4):
            n = A_U if p < 2 else B_U
            u = H_OFF[p]
            WC[o, 2 * u : 2 * u + n] = gate[:, u : u + n]
            WC[o, 2 * u + n : 2 * u + 2 * n] = up[:, u : u + n]

    def project(t):
        arrive(f"gc{t}", G[t].at[0:8], sib)
        if t == 0:
            loads[3].wait()
        L = 2 * NR[t]
        rows = G[t][...].reshape(8 * L, 1024)
        part = jnp.dot(rows, WO[...], preferred_element_type=F32).astype(BF).reshape(8, L, 512)
        for j in range(8):
            PP[t][place(j)] = part[j]
        if t == len(NR) - 1:
            send("s_dw", dw.at[other, :], DD.at[1], sib)
        if t in TWO_HOPS:
            for n in (1, 3, 2):
                pair = pl.ds(2 * ((z + n) % 4), 2)
                send(f"o{t}", PP[t].at[pair], RB[t].at[2 * n - 2 : 2 * n], zdev(n))
            return
        for k in range(1, 8):
            send(f"o{t}", PP[t].at[place((h + k) % 8)], RB[t].at[k - 1], hdev(k))

    def z_sum(t, e):
        total = PP[t][2 * z + e].astype(F32)
        for n in range(3):
            total = total + RB[t][2 * n + e].astype(F32)
        return total

    def other_half(t):
        arrive(f"o{t}", RB[t].at[0:6], hdev(1))
        OS[t][...] = z_sum(t, 1 - xl).astype(BF)
        send(f"ox{t}", OS[t], OXR[t], hdev(4))

    def combine(t):
        if t == 0:
            loads[4].wait()
        r0, nr = ROW0[t], NR[t]
        rows = (slice(r0, r0 + nr), slice(64 + r0, 64 + r0 + nr))
        total = jnp.concatenate([RES[r, :] for r in rows], axis=0).astype(F32)
        if t in TWO_HOPS:
            total = total + z_sum(t, xl)
            arrive(f"ox{t}", OXR[t], hdev(4))
            total = total + OXR[t][...].astype(F32)
        else:
            total = total + PP[t][place(h)].astype(F32)
            arrive(f"o{t}", RB[t], hdev(1))
            for k in range(7):
                total = total + RB[t][k].astype(F32)
        rounded = total.astype(BF)
        own = X[t].at[place(h), :, 0:512]
        own[...] = rounded
        if t in TWO_HOPS:
            send(f"xx_{t}", own, own, hdev(4))
        else:
            for k in range(1, 8):
                send(f"x{t}{k}", own, own, hdev(k))
        send(f"xc{t}", own, X[t].at[place(h), :, 512:1024], sib)
        out[0, rows[0], :] = rounded[0:nr]
        out[0, rows[1], :] = rounded[nr : 2 * nr]

    def spread_pair(t):
        one = 2 * z + 1 - xl
        arrive(f"xx_{t}", X[t].at[one, :, 0:512], hdev(4))
        both = X[t].at[pl.ds(2 * z, 2), :, 0:512]
        for n in (1, 3, 2):
            send(f"x{t}{n}", both, both, zdev(n))
        send(f"xc{t}", X[t].at[one, :, 0:512], X[t].at[one, :, 512:1024], sib)

    def spread(t, k):
        if t in TWO_HOPS:
            j = pl.ds(2 * ((z + 4 - k) % 4), 2)
            arrive(f"x{t}{k}", X[t].at[j, :, 0:512], zdev(4 - k))
        else:
            j = place((h + 8 - k) % 8)
            arrive(f"x{t}{k}", X[t].at[j, :, 0:512], hdev(8 - k))
        send(f"xc{t}", X[t].at[j, :, 0:512], X[t].at[j, :, 512:1024], sib)

    def spread_end(t):
        arrive(f"xc{t}", X[t].at[:, :, 512:1024], sib)

    step_dev = [wdev(0, 1), wdev(0, 3)]
    from_dev = [wdev(0, 3), wdev(0, 1)]
    xdev = wdev(1, 0)

    def first(d, s):
        return (y + 3 - s + 4) % 4 if d == 0 else (y + 1 + s) % 4

    def product(t, out, col0, width):
        @pl.loop(0, width // 256)
        def _(i):
            rows = X[t][...].reshape(16 * NR[t], 1024)
            cols = pl.ds(pl.multiple_of(col0 + i * 256, 256), 256)
            part = jnp.dot(rows, WC[:, cols], preferred_element_type=F32).astype(BF)
            out[:, :, :, pl.ds(pl.multiple_of(i * 256, 256), 256)] = part.reshape(4, 2, 2 * NR[t], 256)

    def a_piece(t, d):
        product(t, PA[t].at[d], d * A_W, A_W)
        send(f"a{t}{d}0", PA[t].at[d, first(d, 0)], RA[t].at[d, 0], step_dev[d])

    def b_piece(t, d):
        product(t, PB[t].at[d], 2 * A_W + d * B_W, B_W)
        for s in range(4):
            g = first(d, s)
            send(f"bx{t}{d}{s}", PB[t].at[d, g, xo], RBX[t].at[d, s], xdev)

    def squares(t):
        ones = jnp.ones((8, 1024), BF)
        for b in range(8):
            v = X[t][b].astype(F32)
            part = lax.dot_general(
                ones, (v * v).astype(BF), (((1,), (1,)), ((), ())), preferred_element_type=F32
            )
            SQ[t][b] = jnp.concatenate([part] * (64 // NR[t]), axis=1)
        for n, (dx, dy) in enumerate(OTHERS):
            b = ((y + dy) % 4) * 2 + (xh + dx) % 2
            send(f"q{t}", SQ[t].at[b], SQR[t].at[n], wdev(dx, dy))

    def row_scale(t):
        total = SQ[t][y * 2 + xh]
        arrive(f"q{t}", SQR[t], wdev(0, 1))
        for n in range(7):
            total = total + SQR[t][n]
        scale = lax.rsqrt(jnp.transpose(total)[0 : 2 * NR[t], 0:1] / D + epsilon)
        SC[t][...] = jnp.broadcast_to(scale, (2 * NR[t], 128))

    def add(out, left, right):
        for i in range(out.shape[0] // 32):
            r = slice(32 * i, 32 * i + 32)
            out[r, :] = (left[r, :].astype(F32) + right[r, :].astype(F32)).astype(BF)

    def a_step(t, d, s):
        g = first(d, s)
        arrive(f"a{t}{d}{s - 1}", RA[t].at[d, s - 1], from_dev[d])
        for e in range(2):
            add(PA[t].at[d, g, e], PA[t].at[d, g, e], RA[t].at[d, s - 1, e])
        if s < 3:
            send(f"a{t}{d}{s}", PA[t].at[d, g], RA[t].at[d, s], step_dev[d])
        else:
            send(f"xx{t}{d}", PA[t].at[d, y, xo], RAX[t].at[d], xdev)

    def b_sum(t, d, s):
        g = first(d, s)
        out = PB[t].at[d, g, xh]
        arrive(f"bx{t}{d}{s}", RBX[t].at[d, s], xdev)
        add(out, out, RBX[t].at[d, s])
        if s and s < 3:
            arrive(f"b{t}{d}{s - 1}", RBY[t].at[d, s - 1], from_dev[d])
            add(out, out, RBY[t].at[d, s - 1])
        if s < 3:
            send(f"b{t}{d}{s}", out, RBY[t].at[d, s], step_dev[d])

    def gated(t, left, right, n, col0):
        scale = SC[t][:, 0:1]
        gate = (left[:, 0:n].astype(F32) + right[:, 0:n].astype(F32)) * scale
        up = (left[:, n : 2 * n].astype(F32) + right[:, n : 2 * n].astype(F32)) * scale
        H[t][y, xh, :, col0 : col0 + n] = (gate / (1.0 + jnp.exp(-gate)) * up).astype(BF)

    def cols(part, d):
        o = H_OFF[2 * part + d]
        return slice(o, o + (A_U, B_U)[part])

    def b_end(t, d):
        b_sum(t, d, 3)
        arrive(f"b{t}{d}2", RBY[t].at[d, 2], from_dev[d])
        gated(t, PB[t].at[d, y, xh], RBY[t].at[d, 2], B_U, H_OFF[2 + d])
        piece = H[t].at[y, xh, :, cols(1, d)]
        send(f"hb{t}{d}0", piece, piece, step_dev[d])
        send(f"hx{t}{d}9", piece, piece, xdev)

    def hb_step(t, d, s):
        piece = H[t].at[first(d, s), xh, :, cols(1, d)]
        arrive(f"hb{t}{d}{s}", piece, from_dev[d])
        if s < 2:
            send(f"hb{t}{d}{s + 1}", piece, piece, step_dev[d])
        send(f"hx{t}{d}{s}", piece, piece, xdev)

    def a_end(t, d):
        arrive(f"xx{t}{d}", RAX[t].at[d], xdev)
        gated(t, PA[t].at[d, y, xh], RAX[t].at[d], A_U, H_OFF[d])
        piece = H[t].at[y, xh, :, cols(0, d)]
        send(f"ho{t}{d}0", piece, piece, step_dev[d])
        send(f"hp{t}{d}9", piece, piece, xdev)

    def ha_step(t, d, s, q):
        if s == 9:
            piece = H[t].at[y, xo, :, cols(0, d)]
            arrive(f"hp{t}{d}9", piece, xdev)
            send(f"hp{t}{d}0", piece, piece, step_dev[d])
            return
        piece = H[t].at[first(d, s), xh if q == "o" else xo, :, cols(0, d)]
        arrive(f"h{q}{t}{d}{s}", piece, from_dev[d])
        if s < 2:
            send(f"h{q}{t}{d}{s + 1}", piece, piece, step_dev[d])

    down_ready = []

    def down(t, i):
        if not down_ready:
            loads[5].wait()
            arrive("s_dw", DD.at[1], sib)
            down_ready.append(True)
        steps = ((9,), (1,), (0, 2))[i]
        for s in steps:
            for d in range(2):
                g = y if s == 9 else first(d, s)
                arrive(f"hx{t}{d}{s}", H[t].at[g, xo, :, cols(1, d)], xdev)
                if s == 2:
                    ha_step(t, d, 2, "o")
                    ha_step(t, d, 2, "p")
        gs = ((y,), ((y + 2) % 4,), ((y + 1) % 4, (y + 3) % 4))[i]
        for e, out in ((1, PDS), (0, PDO)):
            @pl.loop(0, 2)
            def _(n):
                n = pl.ds(pl.multiple_of(n * 256, 256), 256)
                rows = jnp.concatenate([H[t][g].reshape(4 * NR[t], HALF) for g in gs], axis=0)
                part = jnp.dot(rows, DD[e, :, n], preferred_element_type=F32).astype(BF)
                for m, g in enumerate(gs):
                    block = part[4 * NR[t] * m : 4 * NR[t] * (m + 1)].reshape(2, 2 * NR[t], 256)
                    out[t][pl.ds(2 * g, 2), :, n] = block

            if e:
                for m, g in enumerate(gs):
                    pair = pl.ds(2 * g, 2)
                    send(f"sh{t}{i}{m}", PDS[t].at[pair], PDI[t].at[pair], sib)

    def down_whole(t):
        for s in (9, 1, 0, 2):
            for d in range(2):
                g = y if s == 9 else first(d, s)
                arrive(f"hx{t}{d}{s}", H[t].at[g, xo, :, cols(1, d)], xdev)
                if s == 2:
                    ha_step(t, d, 2, "o")
                    ha_step(t, d, 2, "p")
        for e, to in ((1, PDS), (0, PDO)):
            @pl.loop(0, 2)
            def _(n):
                n = pl.ds(pl.multiple_of(n * 256, 256), 256)
                rows = H[t][...].reshape(16 * NR[t], HALF)
                part = jnp.dot(rows, DD[e, :, n], preferred_element_type=F32).astype(BF)
                to[t][:, :, n] = part.reshape(8, 2 * NR[t], 256)

            if e:
                send(f"sh{t}", PDS[t], PDI[t], sib)

    def share_whole(t):
        arrive(f"sh{t}", PDI[t], sib)
        for k in range(1, 9):
            j = place((h + k) % 8)
            add(PDO[t].at[j], PDO[t].at[j], PDI[t].at[j])
            if k < 8:
                send(f"f{t}", PDO[t].at[j], FR[t].at[k - 1], hdev(k))

    def share(t, i):
        gs = ((y,), ((y + 2) % 4,), ((y + 1) % 4, (y + 3) % 4))[i]
        index = names.setdefault(f"f{t}", len(names))
        for m, g in enumerate(gs):
            pair = pl.ds(2 * g, 2)
            arrive(f"sh{t}{i}{m}", PDI[t].at[pair], sib)
            for e in range(2):
                j = 2 * g + e
                add(PDO[t].at[j], PDO[t].at[j], PDI[t].at[j])

            @pl.when(g != z)
            def _():
                slot = (g - z + 4) % 4 - 1
                copy_of(index, PDO[t].at[pair], FR[t].at[pl.ds(2 * slot, 2)], (xl * 4 + g, w)).start()

    def head_sum(t, e):
        total = PDO[t][2 * z + e].astype(F32)
        for n in range(3):
            total = total + FR[t][2 * n + e].astype(F32)
        return total

    def across(t):
        arrive(f"f{t}", FR[t].at[0:6], hdev(1))
        for n in range(1, 4):
            g = (z + n) % 4
            sent.append(
                copy_of(names[f"f{t}"], PDO[t].at[pl.ds(2 * g, 2)], FR[t].at[2 * n - 2 : 2 * n], (xl * 4 + g, w))
            )
        FS[t][...] = head_sum(t, 1 - xl).astype(BF)
        send(f"fx{t}", FS[t], FXR[t], hdev(4))

    def finish(t):
        if t == LAST:
            arrive(f"f{t}", FR[t], hdev(1))
            total = PDO[t][place(h)].astype(F32)
            for n in range(7):
                total = total + FR[t][n].astype(F32)
        else:
            total = head_sum(t, xl)
            arrive(f"fx{t}", FXR[t], hdev(4))
            total = total + FXR[t][...].astype(F32)
        rounded = total.astype(BF)
        r0, nr = ROW0[t], NR[t]
        out[1, r0 : r0 + nr, :] = rounded[0:nr]
        out[1, 64 + r0 : 64 + r0 + nr, :] = rounded[nr : 2 * nr]

    steps = {"in": (enter,)}
    for k in range(16):
        steps[f"u{k}"] = (untwist, k)
    for t in range(len(NR)):
        steps[f"at{t}"] = (attend, t)
        for dx, dy in OTHERS:
            steps[f"gf{t}{dx}{dy}"] = (gather_on, t, dx, dy)
        steps[f"op{t}"] = (project, t)
        steps[f"cm{t}"] = (combine, t)
        if t in TWO_HOPS:
            steps[f"or{t}"] = (other_half, t)
            steps[f"xp{t}"] = (spread_pair, t)
        for k in range(1, 4 if t in TWO_HOPS else 8):
            steps[f"xf{t}{k}"] = (spread, t, k)
        steps[f"xr{t}"] = (spread_end, t)
        steps[f"sq{t}"] = (squares, t)
        steps[f"sc{t}"] = (row_scale, t)
        for d in range(2):
            steps[f"ga{t}{d}"] = (a_piece, t, d)
            steps[f"gb{t}{d}"] = (b_piece, t, d)
            for s in range(3):
                steps[f"as{t}{d}{s + 1}"] = (a_step, t, d, s + 1)
                steps[f"bs{t}{d}{s}"] = (b_sum, t, d, s)
                steps[f"hb{t}{d}{s}"] = (hb_step, t, d, s)
            steps[f"bf{t}{d}"] = (b_end, t, d)
            steps[f"af{t}{d}"] = (a_end, t, d)
            for s in (0, 1):
                for q in "op":
                    steps[f"h{q}{t}{d}{s}"] = (ha_step, t, d, s, q)
            steps[f"hp{t}{d}9"] = (ha_step, t, d, 9, "p")
        if t == LAST:
            steps[f"dn{t}"] = (down_whole, t)
            steps[f"fz{t}"] = (share_whole, t)
        else:
            for i in range(3):
                steps[f"dn{t}{i}"] = (down, t, i)
                steps[f"fz{t}{i}"] = (share, t, i)
            steps[f"fx{t}"] = (across, t)
        steps[f"fo{t}"] = (finish, t)
    table = list(steps.values())
    assert sorted(ORDER) == list(range(len(table)))
    for number in ORDER:
        step, *where = table[number]
        step(*where)

    assert len(names) <= N_COPIES
    for cp in sent:
        cp.wait_send()


N_COPIES = 224


def layer(
    queries, fresh_keys, fresh_values, cached_keys, cached_values, context_len, tree_size, parents,
    residual, out_weight, gate_up_weight, down_weight,
):
    vm = pltpu.VMEM

    def parts(per_row, *shape):
        return tuple(vm(tuple(x or per_row * n for x in shape), BF) for n in NR)

    scratch = [
        vm((CTX, HD), BF),
        vm((CTX, HD), BF),
        vm((128, HD), BF),
        vm((128, HD), BF),
        vm((256, CTX + 128), F32),
        vm((256, CTX + 128), BF),
        vm((TREE, 128), F32),
        parts(1, 0, 1024),
        parts(1, 16, 0, 1024),
        vm((512, 2, HALF), BF),
        vm((512, 2, HALF), BF),
        vm((1024, 2 * HALF), BF),
        vm((2, HALF, 512), BF),
        vm((1024, 512), BF),
        vm((128, 512), BF),
        parts(2, 8, 0, 512),
        parts(2, 7, 0, 512),
        parts(2, 8, 0, 1024),
        parts(2, 2, 4, 2, 0, A_W),
        parts(2, 2, 4, 2, 0, B_W),
        parts(2, 2, 3, 2, 0, A_W),
        parts(2, 2, 0, A_W),
        parts(2, 2, 4, 0, B_W),
        parts(2, 2, 3, 0, B_W),
        tuple(vm((8, 8, 128), F32) for n in NR),
        tuple(vm((7, 8, 128), F32) for n in NR),
        tuple(vm((2 * n, 128), F32) for n in NR),
        parts(2, 4, 2, 0, HALF),
        parts(2, 8, 0, 512),
        parts(2, 8, 0, 512),
        parts(2, 8, 0, 512),
        parts(2, 7, 0, 512),
        parts(2, 0, 512),
        parts(2, 0, 512),
        parts(2, 0, 512),
        parts(2, 0, 512),
        pltpu.SemaphoreType.DMA((6,)),
        pltpu.SemaphoreType.DMA((1,)),
        pltpu.SemaphoreType.DMA((N_COPIES,)),
    ]
    in_vmem = pl.BlockSpec(memory_space=pltpu.VMEM)
    in_smem = pl.BlockSpec(memory_space=pltpu.SMEM)
    in_hbm = pl.BlockSpec(memory_space=pl.ANY)
    both = pl.pallas_call(
        layer_kernel,
        out_shape=jax.ShapeDtypeStruct((2, 128, 512), BF),
        in_specs=[in_vmem] * 4 + [in_smem] * 2 + [in_hbm] * 6,
        out_specs=in_vmem,
        scratch_shapes=scratch,
        name="layer",
        compiler_params=pltpu.CompilerParams(
            collective_id=0, has_side_effects=True, vmem_limit_bytes=60 << 20
        ),
    )(
        queries, fresh_keys, fresh_values, parents, context_len, tree_size, cached_keys, cached_values,
        gate_up_weight, down_weight, out_weight, residual,
    )
    return both[0], both[1]


def solution(mesh):
    placed = (
        P("wide", "head"),
        P("wide", "head"),
        P("wide", "head"),
        P("wide", None, "head"),
        P("wide", None, "head"),
        P("wide"),
        P("wide"),
        P("wide", None),
        P(None, "wide"),
        P("head", "wide"),
        P("wide", None, "head"),
        P("head", "wide"),
    )
    return jax.shard_map(
        layer,
        mesh=mesh,
        in_specs=placed,
        out_specs=(P("head", "wide"), P("head", "wide")),
        check_vma=False,
    )
```

```python
import math

import jax
import jax.numpy as jnp
from jax import lax
from jax.experimental import pallas as pl
from jax.experimental.pallas import tpu as pltpu
from jax.sharding import PartitionSpec as P

D = 8192
HD = 128
CTX = 2048
TREE = 64

epsilon = 1e-05

BF = jnp.bfloat16
F32 = jnp.float32
MESH = pl.DeviceIdType.MESH

A_U = 512
B_U = 384
A_W = 2 * A_U
B_W = 2 * B_U
HALF = 2 * A_U + 2 * B_U
H_OFF = (0, A_U, 2 * A_U, 2 * A_U + B_U)
OTHERS = ((0, 1), (0, 3), (1, 0), (0, 2), (1, 1), (1, 3), (1, 2))

NR = (16, 32, 16)
ROW0 = (0, 16, 48)
LAST = len(NR) - 1
TWO_HOPS = ()

ORDER = (
    0, 17, 81, 145, 22, 20, 1, 2, 19, 23, 21, 82, 18, 24, 3, 4, 25, 85, 83, 86, 88, 84, 87, 5, 6,
    150, 89, 152, 147, 151, 7, 148, 146, 149, 8, 26, 153, 9, 10, 11, 90, 12, 27, 13, 32, 28, 30, 29,
    31, 14, 33, 15, 16, 34, 37, 56, 92, 55, 95, 91, 93, 94, 96, 97, 38, 39, 58, 98, 101, 57, 154,
    61, 119, 42, 120, 64, 40, 157, 99, 158, 103, 122, 161, 155, 160, 121, 156, 159, 102, 162, 165,
    184, 183, 106, 166, 167, 60, 124, 100, 35, 43, 104, 163, 186, 170, 109, 168, 125, 185, 127, 107,
    46, 128, 63, 113, 188, 189, 36, 173, 45, 110, 130, 67, 114, 131, 164, 171, 191, 112, 177, 192,
    123, 118, 48, 132, 49, 105, 66, 136, 174, 195, 194, 115, 126, 137, 108, 133, 41, 182, 176, 116,
    50, 134, 54, 111, 129, 59, 72, 187, 44, 68, 200, 73, 135, 169, 62, 117, 139, 138, 69, 52, 178,
    196, 190, 47, 51, 197, 172, 70, 179, 140, 141, 53, 71, 198, 180, 65, 193, 75, 199, 181, 175,
    142, 77, 201, 76, 78, 74, 143, 202, 79, 144, 203, 80,
)


def layer_kernel(
    queries, fresh_k, fresh_v, parents, length, live, keys_hbm, values_hbm,
    gw, dw, wo_hbm, res_hbm,
    out,
    KS, VS, FK, FV, S, PR, TB, ATT,
    G, R0, R1, WC, DD, WO, RES, PP, RB, X, PA, PB, RA, RAX, RBX, RBY, SQ, SQR, SC, H, PDO, PDS, PDI, FR, FS, FXR, OS, OXR,
    lsem, ssem, rsem,
):
    h = lax.axis_index("head")
    w = lax.axis_index("wide")
    xh = w // 8
    y = (w // 2) % 4
    c = w % 2
    flip = 1 - 2 * c
    xo = 1 - xh

    def wide(dxh, dy):
        return (((xh + dxh + 2) % 2) * 4 + (y + dy + 4) % 4) * 2 + c

    sib = (h, w + flip)
    xl = h // 4
    z = h % 4

    def place(j):
        return 2 * (j % 4) + j // 4

    def wdev(dxh, dy):
        return (h, wide(dxh, dy))

    def hdev(k):
        return ((h + k) % 8, w)

    def zdev(n):
        return (xl * 4 + (z + n) % 4, w)

    names = {}
    sent = []

    def copy_of(i, src, dst, dev):
        return pltpu.make_async_remote_copy(
            src_ref=src, dst_ref=dst, send_sem=ssem.at[0], recv_sem=rsem.at[i],
            device_id=dev, device_id_type=MESH,
        )

    def send(name, src, dst, dev):
        i = names.setdefault(name, len(names))
        cp = copy_of(i, src, dst, dev)
        cp.start()
        sent.append(cp)

    def arrive(name, dst, dev):
        copy_of(names[name], dst, dst, dev).wait_recv()

    mine = pl.ds(pl.multiple_of(c * HALF, 128), HALF)
    other = pl.ds(pl.multiple_of((1 - c) * HALF, 128), HALF)
    loads = [
        pltpu.make_async_copy(keys_hbm.at[0], KS, lsem.at[0]),
        pltpu.make_async_copy(values_hbm.at[0], VS, lsem.at[1]),
        pltpu.make_async_copy(gw.at[:, :, mine], R0, lsem.at[2]),
        pltpu.make_async_copy(wo_hbm, WO, lsem.at[3]),
        pltpu.make_async_copy(
            res_hbm.at[pl.ds(pl.multiple_of(h * 128, 128), 128), :], RES, lsem.at[4]
        ),
        pltpu.make_async_copy(dw.at[mine, :], DD.at[0], lsem.at[5]),
    ]
    for cp in loads:
        cp.start()

    partners = [sib]
    partners += [wdev(dx, dy) for dx, dy in OTHERS]
    partners += [hdev(k) for k in range(1, 8)]
    barrier = pltpu.get_barrier_semaphore()
    for dev in partners:
        pl.semaphore_signal(barrier, inc=1, device_id=dev, device_id_type=MESH)

    def enter():
        pl.semaphore_wait(barrier, len(partners))
        send("s_gw", gw.at[:, :, other], R1, sib)

    node = lax.broadcasted_iota(jnp.int32, (TREE, TREE), 0)
    child = lax.broadcasted_iota(jnp.int32, (TREE, TREE), 1)
    linked = (parents[...] == node) | (node == child)
    reached = jnp.where(linked, 1.0, 0.0).astype(BF)
    for squaring in range(6):
        reached = jnp.minimum(jnp.dot(reached, reached, preferred_element_type=F32), 1.0).astype(BF)
    same = jnp.where(node == child, 1.0, 0.0).astype(BF)
    visible = lax.dot_general(reached, same, (((0,), (0,)), ((), ())), preferred_element_type=F32)
    TB[...] = jnp.full((TREE, 128), -1e30, F32)
    TB[:, 0:TREE] = jnp.where((visible > 0.5) & (child < live[0]), 0.0, -1e30)
    FK[0:TREE] = fresh_k[...]
    FK[TREE:128] = jnp.zeros((128 - TREE, HD), BF)
    FV[0:TREE] = fresh_v[...]
    FV[TREE:128] = jnp.zeros((128 - TREE, HD), BF)
    positions = lax.broadcasted_iota(jnp.int32, (1, CTX), 1)
    cache_bias = jnp.where(positions < length[0], 0.0, -1e30)
    score_scale = math.log2(math.e) / math.sqrt(HD)

    def attend(t):
        if t == 0:
            loads[0].wait()
        r0, nr = ROW0[t], NR[t]
        m8 = 8 * nr
        q = jnp.concatenate([queries[r0 : r0 + nr, j * HD : (j + 1) * HD] for j in range(8)], axis=0)
        trans = (((1,), (1,)), ((), ()))

        @pl.loop(0, CTX // 512)
        def _(i):
            n = pl.ds(pl.multiple_of(i * 512, 512), 512)
            S[0:m8, n] = lax.dot_general(q, KS[n, :], trans, preferred_element_type=F32)

        S[0:m8, CTX : CTX + 128] = lax.dot_general(q, FK[...], trans, preferred_element_type=F32)
        if t == 0:
            loads[1].wait()
        alive = lax.broadcasted_iota(jnp.int32, (nr, 1), 0) + r0 < live[0]
        denominators = []
        strips = nr // 16
        for j in range(8 * strips):
            r = slice(16 * j, 16 * j + 16)
            n0 = r0 + 16 * (j % strips)
            cache = S[r, 0:CTX] + cache_bias
            tree = S[r, CTX : CTX + 128] + TB[n0 : n0 + 16, :]
            row_max = jnp.maximum(
                jnp.max(cache, axis=1, keepdims=True), jnp.max(tree, axis=1, keepdims=True)
            )
            cache = jnp.exp2((cache - row_max) * score_scale)
            tree = jnp.exp2((tree - row_max) * score_scale)
            denominators.append(
                jnp.sum(cache, axis=1, keepdims=True) + jnp.sum(tree, axis=1, keepdims=True)
            )
            PR[r, 0:CTX] = cache.astype(BF)
            PR[r, CTX : CTX + 128] = tree.astype(BF)
        mixed = jnp.dot(PR[0:m8, 0:CTX], VS[...], preferred_element_type=F32)
        mixed = mixed + jnp.dot(PR[0:m8, CTX : CTX + 128], FV[...], preferred_element_type=F32)
        for j in range(8):
            below = jnp.concatenate(denominators[strips * j : strips * j + strips], axis=0)
            part = mixed[nr * j : nr * j + nr] / below
            ATT[t][:, j * HD : (j + 1) * HD] = jnp.where(alive, part, 0.0).astype(BF)
        for dx, dy in OTHERS:
            send(f"g{t}{dx}{dy}", ATT[t], G[t].at[w], wdev(dx, dy))
        send(f"gc{t}", ATT[t], G[t].at[w], sib)
        G[t][w] = ATT[t][...]

    def gather_on(t, dx, dy):
        src = wide(-dx, -dy)
        arrive(f"g{t}{dx}{dy}", G[t].at[src], wdev(-dx, -dy))
        send(f"gc{t}", G[t].at[src], G[t].at[src], sib)

    def untwist(k):
        if k == 0:
            loads[2].wait()
        if k == 8:
            arrive("s_gw", R1, sib)
        raw = R0 if k < 8 else R1
        i = k % 8
        b = raw[64 * i : 64 * i + 64]
        gate, up = b[:, 0, :], b[:, 1, :]
        o = slice(64 * k, 64 * k + 64)
        for p in range(4):
            n = A_U if p < 2 else B_U
            u = H_OFF[p]
            WC[o, 2 * u : 2 * u + n] = gate[:, u : u + n]
            WC[o, 2 * u + n : 2 * u + 2 * n] = up[:, u : u + n]

    def project(t):
        arrive(f"gc{t}", G[t].at[0:8], sib)
        if t == 0:
            loads[3].wait()
        L = 2 * NR[t]
        rows = G[t][...].reshape(8 * L, 1024)
        part = jnp.dot(rows, WO[...], preferred_element_type=F32).astype(BF).reshape(8, L, 512)
        for j in range(8):
            PP[t][place(j)] = part[j]
        if t == len(NR) - 1:
            send("s_dw", dw.at[other, :], DD.at[1], sib)
        if t in TWO_HOPS:
            for n in (1, 3, 2):
                pair = pl.ds(2 * ((z + n) % 4), 2)
                send(f"o{t}", PP[t].at[pair], RB[t].at[2 * n - 2 : 2 * n], zdev(n))
            return
        for k in range(1, 8):
            send(f"o{t}", PP[t].at[place((h + k) % 8)], RB[t].at[k - 1], hdev(k))

    def z_sum(t, e):
        total = PP[t][2 * z + e].astype(F32)
        for n in range(3):
            total = total + RB[t][2 * n + e].astype(F32)
        return total

    def other_half(t):
        arrive(f"o{t}", RB[t].at[0:6], hdev(1))
        OS[t][...] = z_sum(t, 1 - xl).astype(BF)
        send(f"ox{t}", OS[t], OXR[t], hdev(4))

    def combine(t):
        if t == 0:
            loads[4].wait()
        r0, nr = ROW0[t], NR[t]
        rows = (slice(r0, r0 + nr), slice(64 + r0, 64 + r0 + nr))
        total = jnp.concatenate([RES[r, :] for r in rows], axis=0).astype(F32)
        if t in TWO_HOPS:
            total = total + z_sum(t, xl)
            arrive(f"ox{t}", OXR[t], hdev(4))
            total = total + OXR[t][...].astype(F32)
        else:
            total = total + PP[t][place(h)].astype(F32)
            arrive(f"o{t}", RB[t], hdev(1))
            for k in range(7):
                total = total + RB[t][k].astype(F32)
        rounded = total.astype(BF)
        own = X[t].at[place(h), :, 0:512]
        own[...] = rounded
        if t in TWO_HOPS:
            send(f"xx_{t}", own, own, hdev(4))
        else:
            for k in range(1, 8):
                send(f"x{t}{k}", own, own, hdev(k))
        send(f"xc{t}", own, X[t].at[place(h), :, 512:1024], sib)
        out[0, rows[0], :] = rounded[0:nr]
        out[0, rows[1], :] = rounded[nr : 2 * nr]

    def spread_pair(t):
        one = 2 * z + 1 - xl
        arrive(f"xx_{t}", X[t].at[one, :, 0:512], hdev(4))
        both = X[t].at[pl.ds(2 * z, 2), :, 0:512]
        for n in (1, 3, 2):
            send(f"x{t}{n}", both, both, zdev(n))
        send(f"xc{t}", X[t].at[one, :, 0:512], X[t].at[one, :, 512:1024], sib)

    def spread(t, k):
        if t in TWO_HOPS:
            j = pl.ds(2 * ((z + 4 - k) % 4), 2)
            arrive(f"x{t}{k}", X[t].at[j, :, 0:512], zdev(4 - k))
        else:
            j = place((h + 8 - k) % 8)
            arrive(f"x{t}{k}", X[t].at[j, :, 0:512], hdev(8 - k))
        send(f"xc{t}", X[t].at[j, :, 0:512], X[t].at[j, :, 512:1024], sib)

    def spread_end(t):
        arrive(f"xc{t}", X[t].at[:, :, 512:1024], sib)

    step_dev = [wdev(0, 1), wdev(0, 3)]
    from_dev = [wdev(0, 3), wdev(0, 1)]
    xdev = wdev(1, 0)

    def first(d, s):
        return (y + 3 - s + 4) % 4 if d == 0 else (y + 1 + s) % 4

    def product(t, out, col0, width):
        @pl.loop(0, width // 256)
        def _(i):
            rows = X[t][...].reshape(16 * NR[t], 1024)
            cols = pl.ds(pl.multiple_of(col0 + i * 256, 256), 256)
            part = jnp.dot(rows, WC[:, cols], preferred_element_type=F32).astype(BF)
            out[:, :, :, pl.ds(pl.multiple_of(i * 256, 256), 256)] = part.reshape(4, 2, 2 * NR[t], 256)

    def a_piece(t, d):
        product(t, PA[t].at[d], d * A_W, A_W)
        send(f"a{t}{d}0", PA[t].at[d, first(d, 0)], RA[t].at[d, 0], step_dev[d])

    def b_piece(t, d):
        product(t, PB[t].at[d], 2 * A_W + d * B_W, B_W)
        for s in range(4):
            g = first(d, s)
            send(f"bx{t}{d}{s}", PB[t].at[d, g, xo], RBX[t].at[d, s], xdev)

    def squares(t):
        ones = jnp.ones((8, 1024), BF)
        for b in range(8):
            v = X[t][b].astype(F32)
            part = lax.dot_general(
                ones, (v * v).astype(BF), (((1,), (1,)), ((), ())), preferred_element_type=F32
            )
            SQ[t][b] = jnp.concatenate([part] * (64 // NR[t]), axis=1)
        for n, (dx, dy) in enumerate(OTHERS):
            b = ((y + dy) % 4) * 2 + (xh + dx) % 2
            send(f"q{t}", SQ[t].at[b], SQR[t].at[n], wdev(dx, dy))

    def row_scale(t):
        total = SQ[t][y * 2 + xh]
        arrive(f"q{t}", SQR[t], wdev(0, 1))
        for n in range(7):
            total = total + SQR[t][n]
        scale = lax.rsqrt(jnp.transpose(total)[0 : 2 * NR[t], 0:1] / D + epsilon)
        SC[t][...] = jnp.broadcast_to(scale, (2 * NR[t], 128))

    def add(out, left, right):
        for i in range(out.shape[0] // 32):
            r = slice(32 * i, 32 * i + 32)
            out[r, :] = (left[r, :].astype(F32) + right[r, :].astype(F32)).astype(BF)

    def a_step(t, d, s):
        g = first(d, s)
        arrive(f"a{t}{d}{s - 1}", RA[t].at[d, s - 1], from_dev[d])
        for e in range(2):
            add(PA[t].at[d, g, e], PA[t].at[d, g, e], RA[t].at[d, s - 1, e])
        if s < 3:
            send(f"a{t}{d}{s}", PA[t].at[d, g], RA[t].at[d, s], step_dev[d])
        else:
            send(f"xx{t}{d}", PA[t].at[d, y, xo], RAX[t].at[d], xdev)

    def b_sum(t, d, s):
        g = first(d, s)
        out = PB[t].at[d, g, xh]
        arrive(f"bx{t}{d}{s}", RBX[t].at[d, s], xdev)
        add(out, out, RBX[t].at[d, s])
        if s and s < 3:
            arrive(f"b{t}{d}{s - 1}", RBY[t].at[d, s - 1], from_dev[d])
            add(out, out, RBY[t].at[d, s - 1])
        if s < 3:
            send(f"b{t}{d}{s}", out, RBY[t].at[d, s], step_dev[d])

    def gated(t, left, right, n, col0):
        scale = SC[t][:, 0:1]
        gate = (left[:, 0:n].astype(F32) + right[:, 0:n].astype(F32)) * scale
        up = (left[:, n : 2 * n].astype(F32) + right[:, n : 2 * n].astype(F32)) * scale
        H[t][y, xh, :, col0 : col0 + n] = (gate / (1.0 + jnp.exp(-gate)) * up).astype(BF)

    def cols(part, d):
        o = H_OFF[2 * part + d]
        return slice(o, o + (A_U, B_U)[part])

    def b_end(t, d):
        b_sum(t, d, 3)
        arrive(f"b{t}{d}2", RBY[t].at[d, 2], from_dev[d])
        gated(t, PB[t].at[d, y, xh], RBY[t].at[d, 2], B_U, H_OFF[2 + d])
        piece = H[t].at[y, xh, :, cols(1, d)]
        send(f"hb{t}{d}0", piece, piece, step_dev[d])
        send(f"hx{t}9", piece, piece, xdev)

    def hb_step(t, d, s):
        piece = H[t].at[first(d, s), xh, :, cols(1, d)]
        arrive(f"hb{t}{d}{s}", piece, from_dev[d])
        if s < 2:
            send(f"hb{t}{d}{s + 1}", piece, piece, step_dev[d])
        send(f"hx{t}{1 if s == 1 else 2}", piece, piece, xdev)

    def a_end(t, d):
        arrive(f"xx{t}{d}", RAX[t].at[d], xdev)
        gated(t, PA[t].at[d, y, xh], RAX[t].at[d], A_U, H_OFF[d])
        piece = H[t].at[y, xh, :, cols(0, d)]
        send(f"ho{t}{d}0", piece, piece, step_dev[d])
        send(f"hp{t}{d}9", piece, piece, xdev)

    def ha_step(t, d, s, q):
        if s == 9:
            piece = H[t].at[y, xo, :, cols(0, d)]
            arrive(f"hp{t}{d}9", piece, xdev)
            send(f"hp{t}{d}0", piece, piece, step_dev[d])
            return
        piece = H[t].at[first(d, s), xh if q == "o" else xo, :, cols(0, d)]
        arrive(f"h{q}{t}{d}{s}", piece, from_dev[d])
        if s < 2:
            send(f"h{q}{t}{d}{s + 1}", piece, piece, step_dev[d])

    down_ready = []

    def b_arrive(t, s):
        groups = pl.ds(0, 2) if s == 2 else pl.ds(y if s == 9 else first(0, 1), 1)
        arrive(f"hx{t}{s}", H[t].at[groups, xo, :, 2 * A_U : HALF], xdev)

    def down(t, i):
        if not down_ready:
            loads[5].wait()
            arrive("s_dw", DD.at[1], sib)
            down_ready.append(True)
        steps = ((9,), (1,), (0, 2))[i]
        b_arrive(t, steps[-1])
        for s in steps:
            for d in range(2):
                if s == 2:
                    ha_step(t, d, 2, "o")
                    ha_step(t, d, 2, "p")
        gs = ((y,), ((y + 2) % 4,), ((y + 1) % 4, (y + 3) % 4))[i]
        for e, out in ((1, PDS), (0, PDO)):
            @pl.loop(0, 2)
            def _(n):
                n = pl.ds(pl.multiple_of(n * 256, 256), 256)
                rows = jnp.concatenate([H[t][g].reshape(4 * NR[t], HALF) for g in gs], axis=0)
                part = jnp.dot(rows, DD[e, :, n], preferred_element_type=F32).astype(BF)
                for m, g in enumerate(gs):
                    block = part[4 * NR[t] * m : 4 * NR[t] * (m + 1)].reshape(2, 2 * NR[t], 256)
                    out[t][pl.ds(2 * g, 2), :, n] = block

            if e:
                for m, g in enumerate(gs):
                    pair = pl.ds(2 * g, 2)
                    send(f"sh{t}{i}{m}", PDS[t].at[pair], PDI[t].at[pair], sib)

    def down_whole(t):
        for s in (9, 1, 2):
            b_arrive(t, s)
            for d in range(2):
                if s == 2:
                    ha_step(t, d, 2, "o")
                    ha_step(t, d, 2, "p")
        for e, to in ((1, PDS), (0, PDO)):
            @pl.loop(0, 2)
            def _(n):
                n = pl.ds(pl.multiple_of(n * 256, 256), 256)
                rows = H[t][...].reshape(16 * NR[t], HALF)
                part = jnp.dot(rows, DD[e, :, n], preferred_element_type=F32).astype(BF)
                to[t][:, :, n] = part.reshape(8, 2 * NR[t], 256)

            if e:
                send(f"sh{t}", PDS[t], PDI[t], sib)

    def share_whole(t):
        arrive(f"sh{t}", PDI[t], sib)
        for k in range(1, 9):
            j = place((h + k) % 8)
            add(PDO[t].at[j], PDO[t].at[j], PDI[t].at[j])
            if k < 8:
                send(f"f{t}", PDO[t].at[j], FR[t].at[k - 1], hdev(k))

    def share(t, i):
        gs = ((y,), ((y + 2) % 4,), ((y + 1) % 4, (y + 3) % 4))[i]
        index = names.setdefault(f"f{t}", len(names))
        for m, g in enumerate(gs):
            pair = pl.ds(2 * g, 2)
            arrive(f"sh{t}{i}{m}", PDI[t].at[pair], sib)
            for e in range(2):
                j = 2 * g + e
                add(PDO[t].at[j], PDO[t].at[j], PDI[t].at[j])

            @pl.when(g != z)
            def _():
                slot = (g - z + 4) % 4 - 1
                copy_of(index, PDO[t].at[pair], FR[t].at[pl.ds(2 * slot, 2)], (xl * 4 + g, w)).start()

    def head_sum(t, e):
        total = PDO[t][2 * z + e].astype(F32)
        for n in range(3):
            total = total + FR[t][2 * n + e].astype(F32)
        return total

    def across(t):
        arrive(f"f{t}", FR[t].at[0:6], hdev(1))
        for n in range(1, 4):
            g = (z + n) % 4
            sent.append(
                copy_of(names[f"f{t}"], PDO[t].at[pl.ds(2 * g, 2)], FR[t].at[2 * n - 2 : 2 * n], (xl * 4 + g, w))
            )
        FS[t][...] = head_sum(t, 1 - xl).astype(BF)
        send(f"fx{t}", FS[t], FXR[t], hdev(4))

    def finish(t):
        if t == LAST:
            arrive(f"f{t}", FR[t], hdev(1))
            total = PDO[t][place(h)].astype(F32)
            for n in range(7):
                total = total + FR[t][n].astype(F32)
        else:
            total = head_sum(t, xl)
            arrive(f"fx{t}", FXR[t], hdev(4))
            total = total + FXR[t][...].astype(F32)
        rounded = total.astype(BF)
        r0, nr = ROW0[t], NR[t]
        out[1, r0 : r0 + nr, :] = rounded[0:nr]
        out[1, 64 + r0 : 64 + r0 + nr, :] = rounded[nr : 2 * nr]

    steps = {"in": (enter,)}
    for k in range(16):
        steps[f"u{k}"] = (untwist, k)
    for t in range(len(NR)):
        steps[f"at{t}"] = (attend, t)
        for dx, dy in OTHERS:
            steps[f"gf{t}{dx}{dy}"] = (gather_on, t, dx, dy)
        steps[f"op{t}"] = (project, t)
        steps[f"cm{t}"] = (combine, t)
        if t in TWO_HOPS:
            steps[f"or{t}"] = (other_half, t)
            steps[f"xp{t}"] = (spread_pair, t)
        for k in range(1, 4 if t in TWO_HOPS else 8):
            steps[f"xf{t}{k}"] = (spread, t, k)
        steps[f"xr{t}"] = (spread_end, t)
        steps[f"sq{t}"] = (squares, t)
        steps[f"sc{t}"] = (row_scale, t)
        for d in range(2):
            steps[f"ga{t}{d}"] = (a_piece, t, d)
            steps[f"gb{t}{d}"] = (b_piece, t, d)
            for s in range(3):
                steps[f"as{t}{d}{s + 1}"] = (a_step, t, d, s + 1)
                steps[f"bs{t}{d}{s}"] = (b_sum, t, d, s)
                steps[f"hb{t}{d}{s}"] = (hb_step, t, d, s)
            steps[f"bf{t}{d}"] = (b_end, t, d)
            steps[f"af{t}{d}"] = (a_end, t, d)
            for s in (0, 1):
                for q in "op":
                    steps[f"h{q}{t}{d}{s}"] = (ha_step, t, d, s, q)
            steps[f"hp{t}{d}9"] = (ha_step, t, d, 9, "p")
        if t == LAST:
            steps[f"dn{t}"] = (down_whole, t)
            steps[f"fz{t}"] = (share_whole, t)
        else:
            for i in range(3):
                steps[f"dn{t}{i}"] = (down, t, i)
                steps[f"fz{t}{i}"] = (share, t, i)
            steps[f"fx{t}"] = (across, t)
        steps[f"fo{t}"] = (finish, t)
    table = list(steps.values())
    assert sorted(ORDER) == list(range(len(table)))
    for number in ORDER:
        step, *where = table[number]
        step(*where)

    assert len(names) <= N_COPIES
    for cp in sent:
        cp.wait_send()


N_COPIES = 205


def layer(
    queries, fresh_keys, fresh_values, cached_keys, cached_values, context_len, tree_size, parents,
    residual, out_weight, gate_up_weight, down_weight,
):
    vm = pltpu.VMEM

    def parts(per_row, *shape):
        return tuple(vm(tuple(x or per_row * n for x in shape), BF) for n in NR)

    scratch = [
        vm((CTX, HD), BF),
        vm((CTX, HD), BF),
        vm((128, HD), BF),
        vm((128, HD), BF),
        vm((256, CTX + 128), F32),
        vm((256, CTX + 128), BF),
        vm((TREE, 128), F32),
        parts(1, 0, 1024),
        parts(1, 16, 0, 1024),
        vm((512, 2, HALF), BF),
        vm((512, 2, HALF), BF),
        vm((1024, 2 * HALF), BF),
        vm((2, HALF, 512), BF),
        vm((1024, 512), BF),
        vm((128, 512), BF),
        parts(2, 8, 0, 512),
        parts(2, 7, 0, 512),
        parts(2, 8, 0, 1024),
        parts(2, 2, 4, 2, 0, A_W),
        parts(2, 2, 4, 2, 0, B_W),
        parts(2, 2, 3, 2, 0, A_W),
        parts(2, 2, 0, A_W),
        parts(2, 2, 4, 0, B_W),
        parts(2, 2, 3, 0, B_W),
        tuple(vm((8, 8, 128), F32) for n in NR),
        tuple(vm((7, 8, 128), F32) for n in NR),
        tuple(vm((2 * n, 128), F32) for n in NR),
        parts(2, 4, 2, 0, HALF),
        parts(2, 8, 0, 512),
        parts(2, 8, 0, 512),
        parts(2, 8, 0, 512),
        parts(2, 7, 0, 512),
        parts(2, 0, 512),
        parts(2, 0, 512),
        parts(2, 0, 512),
        parts(2, 0, 512),
        pltpu.SemaphoreType.DMA((6,)),
        pltpu.SemaphoreType.DMA((1,)),
        pltpu.SemaphoreType.DMA((N_COPIES,)),
    ]
    in_vmem = pl.BlockSpec(memory_space=pltpu.VMEM)
    in_smem = pl.BlockSpec(memory_space=pltpu.SMEM)
    in_hbm = pl.BlockSpec(memory_space=pl.ANY)
    both = pl.pallas_call(
        layer_kernel,
        out_shape=jax.ShapeDtypeStruct((2, 128, 512), BF),
        in_specs=[in_vmem] * 4 + [in_smem] * 2 + [in_hbm] * 6,
        out_specs=in_vmem,
        scratch_shapes=scratch,
        name="layer",
        compiler_params=pltpu.CompilerParams(
            collective_id=0, has_side_effects=True, vmem_limit_bytes=60 << 20
        ),
    )(
        queries, fresh_keys, fresh_values, parents, context_len, tree_size, cached_keys, cached_values,
        gate_up_weight, down_weight, out_weight, residual,
    )
    return both[0], both[1]


def solution(mesh):
    placed = (
        P("wide", "head"),
        P("wide", "head"),
        P("wide", "head"),
        P("wide", None, "head"),
        P("wide", None, "head"),
        P("wide"),
        P("wide"),
        P("wide", None),
        P(None, "wide"),
        P("head", "wide"),
        P("wide", None, "head"),
        P("head", "wide"),
    )
    return jax.shard_map(
        layer,
        mesh=mesh,
        in_specs=placed,
        out_specs=(P("head", "wide"), P("head", "wide")),
        check_vma=False,
    )
```
